32 devices in a mesh: seq: 8 (over y, x, core), heads: 4 (over z).
Axes of the slice: x: 2, y: 2, z: 4, core: 2. Of those that a mesh axis runs over, the one named last changes fastest.
Arguments:
- queries: bfloat16 [16384, 2048], P('seq', 'heads'), may hold values from -120 to 120
- keys: bfloat16 [512, 2048], P(None, 'heads'), may hold values from -4.2 to 4.2
- values: bfloat16 [512, 2048], P(None, 'heads'), may hold values from -6 to 6
- out_grad: bfloat16 [16384, 2048], P('seq', 'heads'), may hold values from -6 to 6
- key_proj: bfloat16 [2048, 2048], P(None, 'heads'), may hold values from -0.125 to 0.125
- value_proj: bfloat16 [2048, 2048], P(None, 'heads'), may hold values from -0.125 to 0.125
- global_in: bfloat16 [512, 2048], P('seq', 'heads'), may hold values from -6 to 6
- up_proj: bfloat16 [2048, 8192], P('heads', 'seq'), may hold values from -0.125 to 0.125
- down_proj: bfloat16 [8192, 2048], P('seq', 'heads'), may hold values from -0.0625 to 0.0625
Outputs:
- query_grad: bfloat16 [16384, 2048], P('seq', 'heads')
- global_grad: float32 [512, 2048], P('seq', 'heads')
The draws below stay inside these ranges and needn't reach their ends.
All inputs are finite; a program needn't handle non-finite values.
Results may differ from the reference program's by a relative error of at most 0.014.
Values may be sent and summed in bfloat16 or wider, within the bound.
No kernel may reach another device: no remote copies, remote signals or barrier semaphores. Data moves between devices by JAX's collectives and lax.ppermute only.
A program may use at most 128 MiB of HBM per device.

```python
import jax
import jax.numpy as jnp
from jax import lax

H = 16
HD = 128
D = 2048
F = 8192
G = 512
TOKENS = 16384


def base_keys(key):
    raw = jnp.clip(jax.random.normal(jax.random.fold_in(key, 7), (G, D), jnp.float32), -4.0, 4.0)
    return raw


def draw_keys(key, part):
    return base_keys(key).astype(jnp.bfloat16)


def draw_queries(key, part):
    raw = jnp.clip(jax.random.normal(jax.random.fold_in(key, 5), (TOKENS, D), jnp.float32), -4.0, 4.0)
    return raw.astype(jnp.bfloat16)


def steps_of(stream_key, dims, split, smallest, largest):
    level, own = 1.0, jax.random.fold_in(stream_key, 6)
    for axis_at, shards_of in split:
        heights = jnp.exp(jax.random.uniform(jax.random.fold_in(own, axis_at), (shards_of,), jnp.float32, smallest / len(split), largest / len(split)))
        level = level * jnp.repeat(heights, dims[axis_at] // shards_of).reshape([-1 if axis == axis_at else 1 for axis in range(len(dims))])
    return level


def centred(own_key, dims, spread, reach, split=(), held_as=jnp.bfloat16):
    level = steps_of(own_key, dims, split, -0.22, 0.18) if split else 1.0
    values = jax.random.normal(own_key, dims, jnp.float32) * spread * level
    return jnp.minimum(jnp.maximum(values, -reach), reach).astype(held_as)


def setup_inputs(seed: int = 0) -> dict:
    key_of = jax.random.split(jax.random.key(seed), 10)
    queries = draw_queries(jax.random.fold_in(key_of[9], 71), 0)
    keys = draw_keys(jax.random.fold_in(key_of[9], 71), 0)
    values = centred(key_of[2], (G, D), 1.0, 6.0, ((1, 4),))
    out_grad = centred(key_of[3], (TOKENS, D), 1.0, 6.0, ((0, 8), (1, 4)))
    key_proj = centred(key_of[4], (D, D), D ** -0.5, 0.125, ((1, 4),))
    value_proj = centred(key_of[5], (D, D), D ** -0.5, 0.125, ((1, 4),))
    global_in = centred(key_of[6], (G, D), 1.0, 6.0, ((0, 8), (1, 4)))
    up_proj = centred(key_of[7], (D, F), D ** -0.5, 0.125, ((0, 4), (1, 8)))
    down_proj = centred(key_of[8], (F, D), F ** -0.5, 0.0625, ((0, 8), (1, 4)))
    return {"queries": queries, "keys": keys, "values": values, "out_grad": out_grad, "key_proj": key_proj, "value_proj": value_proj, "global_in": global_in, "up_proj": up_proj, "down_proj": down_proj}


def slope_of(pre):
    return 0.5 * (1.0 + lax.erf(pre * 0.7071067811865476)) + pre * jnp.exp(-0.5 * pre * pre) * 0.3989422804014327


def reference(queries, keys, values, out_grad, key_proj, value_proj, global_in, up_proj, down_proj):
    scale = HD ** -0.5
    tok_count = queries.shape[0]
    query_heads = queries.reshape(tok_count, H, HD).transpose(1, 0, 2)
    grad_heads = out_grad.reshape(tok_count, H, HD).transpose(1, 0, 2)
    key_heads = keys.reshape(G, H, HD).transpose(1, 0, 2)
    value_heads = values.reshape(G, H, HD).transpose(1, 0, 2)

    def one_head(inputs):
        query_one, key_one, value_one, grad_one = inputs
        scores = scale * jnp.dot(query_one, key_one.T, preferred_element_type=jnp.float32)
        weights = jax.nn.softmax(scores, axis=-1)
        weight_grad = jnp.dot(grad_one, value_one.T, preferred_element_type=jnp.float32)
        centre = jnp.sum(weights * weight_grad, axis=-1, keepdims=True)
        score_grad = (weights * (weight_grad - centre)).astype(jnp.bfloat16)
        weights_low = weights.astype(jnp.bfloat16)
        query_part = (scale * jnp.dot(score_grad, key_one, preferred_element_type=jnp.float32)).astype(jnp.bfloat16)
        key_part = scale * jnp.dot(score_grad.T, query_one, preferred_element_type=jnp.float32)
        value_part = jnp.dot(weights_low.T, grad_one, preferred_element_type=jnp.float32)
        return query_part, key_part, value_part

    query_parts, key_parts, value_parts = lax.map(one_head, (query_heads, key_heads, value_heads, grad_heads))
    query_grad = query_parts.transpose(1, 0, 2).reshape(tok_count, D)
    key_low = key_parts.transpose(1, 0, 2).reshape(G, D).astype(jnp.bfloat16)
    value_low = value_parts.transpose(1, 0, 2).reshape(G, D).astype(jnp.bfloat16)
    state_grad = jnp.dot(key_low, key_proj.T, preferred_element_type=jnp.float32) + jnp.dot(value_low, value_proj.T, preferred_element_type=jnp.float32)
    state_low = state_grad.astype(jnp.bfloat16)
    pre = jnp.dot(global_in, up_proj, preferred_element_type=jnp.float32)
    back = jnp.dot(state_low, down_proj.T, preferred_element_type=jnp.float32)
    gated = (slope_of(pre) * back).astype(jnp.bfloat16)
    global_grad = state_grad + jnp.dot(gated, up_proj.T, preferred_element_type=jnp.float32)
    return query_grad, global_grad
```

```python
import functools
import math

import jax
import jax.numpy as jnp
from jax import lax
from jax.experimental import pallas as pl
from jax.experimental.pallas import tpu as pltpu
from jax.sharding import PartitionSpec as P

HD = 128
SCALE = HD**-0.5
SCALE_LOG2 = SCALE * math.log2(math.e)
BF16, F32 = jnp.bfloat16, jnp.float32
NT = (((1,), (1,)), ((), ()))
NN = (((1,), (0,)), ((), ()))
TN = (((0,), (0,)), ((), ()))
VMEM_BYTES = 48 * 2**20


def dot(a, b, dims):
    return lax.dot_general(a, b, dims, preferred_element_type=F32)


def slope_of(pre):
    return (
        0.5 * (1.0 + lax.erf(pre * 0.7071067811865476))
        + pre * jnp.exp(-0.5 * pre * pre) * 0.3989422804014327
    )


def swap(x, axis, distance):
    size = lax.axis_size(axis)
    return lax.ppermute(x, axis, [(i, i ^ distance) for i in range(size)])


def levels_of(first, count):
    levels = []
    while count > 1:
        radix = min(4, count)
        levels.append((first, radix))
        first, count = first * radix, count // radix
    return levels


def gather_blocks(x, axis, first, count):
    blocks = [x]
    for step, radix in levels_of(first, count):
        whole = blocks[0] if len(blocks) == 1 else jnp.stack(blocks)
        got = [swap(whole, axis, step * k) for k in range(1, radix)]
        for other in got:
            blocks = blocks + ([other] if whole is x else list(other))
    return blocks


def scatter_terms(blocks, axis, first, low=BF16):
    levels = levels_of(first, len(blocks))
    for step, radix in reversed(levels[1:]):
        span = step // first
        terms = [blocks[k * span : (k + 1) * span] for k in range(radix)]
        got = [swap(jnp.stack(terms[k]), axis, step * k) for k in range(1, radix)]
        blocks = [
            (terms[0][i].astype(F32) + sum(g[i].astype(F32) for g in got)).astype(low)
            for i in range(span)
        ]
    return [blocks[0]] + [swap(blocks[k], axis, first * k) for k in range(1, len(blocks))]


def attend_kernel(sub, place_ref, q_ref, g_ref, k_ref, v_ref, *rest):
    dq_ref, even_ref, odd_ref, acc_ref, turned_ref = rest[-5:]
    block = pl.program_id(1)

    @pl.when(block == 0)
    def _():
        acc_ref[...] = jnp.zeros_like(acc_ref)

    keys, values = k_ref[...], v_ref[...]
    key_part = value_part = None
    for i in range(q_ref.shape[0] // sub):
        rows = pl.ds(i * sub, sub)
        q, g = q_ref[rows, :], g_ref[rows, :]
        scores = dot(q, keys, NT)
        weight_grad = dot(g, values, NT)
        top = jnp.max(scores, axis=1, keepdims=True)
        grown = jnp.exp2((scores - top) * SCALE_LOG2)
        over = 1.0 / jnp.sum(grown, axis=1, keepdims=True)
        centre = jnp.sum(grown * weight_grad, axis=1, keepdims=True) * over
        weights = grown * over
        score_grad = (weights * (weight_grad - centre)).astype(BF16)
        dq_ref[rows, :] = (SCALE * dot(score_grad, keys, NN)).astype(BF16)
        key_term = dot(q, score_grad, TN)
        value_term = dot(g, weights.astype(BF16), TN)
        key_part = key_term if key_part is None else key_part + key_term
        value_part = value_term if value_part is None else value_part + value_term
    acc_ref[:HD, :] += key_part
    acc_ref[HD:, :] += value_part

    @pl.when(block == pl.num_programs(1) - 1)
    def _():
        turned_ref[:, :HD] = SCALE * acc_ref[:HD, :].T
        turned_ref[:, HD:] = acc_ref[HD:, :].T
        half, height = even_ref.shape[:2]
        for j in range(2 * half):
            at = pl.ds(pl.multiple_of(place_ref[j] * height, height), height)
            (odd_ref if j % 2 else even_ref)[j // 2] = turned_ref[at, :].astype(BF16)


def attend(place, queries, out_grad, keys, values, query_grad, first, count):
    tokens, width = queries.shape
    glob = keys.shape[0]
    size = place.shape[0]
    block = min(512, tokens)
    sub = min(256, block)
    token_spec = pl.BlockSpec((block, HD), lambda h, b, place: (b, h + first))
    global_spec = pl.BlockSpec((glob, HD), lambda h, b, place: (0, h + first))
    part_spec = pl.BlockSpec((size // 2, glob // size, 2 * HD), lambda h, b, place: (0, 0, h))
    part = jax.ShapeDtypeStruct((size // 2, glob // size, 2 * HD * count), BF16)
    operands = [place, queries, out_grad, keys, values]
    specs = [token_spec, token_spec, global_spec, global_spec]
    aliases = {}
    if query_grad is not None:
        operands.append(query_grad)
        specs.append(pl.BlockSpec(memory_space=pl.ANY))
        aliases = {5: 0}
    return pl.pallas_call(
        functools.partial(attend_kernel, sub),
        grid_spec=pltpu.PrefetchScalarGridSpec(
            num_scalar_prefetch=1,
            grid=(count, tokens // block),
            in_specs=specs,
            out_specs=[token_spec, part_spec, part_spec],
            scratch_shapes=[pltpu.VMEM((2 * HD, glob), F32), pltpu.VMEM((glob, 2 * HD), F32)],
        ),
        out_shape=[jax.ShapeDtypeStruct((tokens, width), BF16), part, part],
        input_output_aliases=aliases,
        compiler_params=pltpu.CompilerParams(vmem_limit_bytes=VMEM_BYTES),
        cost_estimate=pl.CostEstimate(
            flops=20 * tokens * glob * HD * count,
            bytes_accessed=6 * tokens * HD * count,
            transcendentals=tokens * glob * count,
        ),
        name="attend",
    )(*operands)


def scatter_rows(even, odd):
    got = swap(odd, "seq", 1)
    mine = (even.astype(F32) + got.astype(F32)).astype(BF16)
    return scatter_terms(list(mine), "seq", 2)


def project_kernel(count, chunk_ref, *refs):
    terms, rest = refs[:count], refs[count:]
    key_proj_ref, value_proj_ref, part_ref = rest[0], rest[1], rest[-1]
    total = sum(t[...].astype(F32) for t in terms).astype(BF16)
    heads = total.shape[1] // (2 * HD)
    pick = lambda at: [total[:, (2 * h + at) * HD : (2 * h + at + 1) * HD] for h in range(heads)]
    key_low, value_low = jnp.concatenate(pick(0), 1), jnp.concatenate(pick(1), 1)
    part = dot(key_low, key_proj_ref[...], NT) + dot(value_low, value_proj_ref[...], NT)
    if len(rest) == 4:
        part = part + rest[2][...]
    part_ref[...] = part


def project(chunk, terms, key_proj, value_proj, first, before):
    rows, width = terms[0].shape
    count = width // (2 * HD)
    size = chunk.shape[0]
    block = key_proj.shape[0] // size
    wide = count * HD
    term_spec = pl.BlockSpec((rows, width), lambda k, chunk: (0, 0))
    weight_spec = pl.BlockSpec((block, wide), lambda k, chunk: (chunk[k], first // count))
    part_spec = pl.BlockSpec((None, rows, block), lambda k, chunk: (k, 0, 0))
    operands = [chunk, *terms, key_proj, value_proj]
    specs = [term_spec] * len(terms) + [weight_spec] * 2
    if before is not None:
        operands.append(before)
        specs.append(part_spec)
    return pl.pallas_call(
        functools.partial(project_kernel, len(terms)),
        grid_spec=pltpu.PrefetchScalarGridSpec(
            num_scalar_prefetch=1, grid=(size,), in_specs=specs, out_specs=part_spec
        ),
        out_shape=jax.ShapeDtypeStruct((size, rows, block), F32),
        compiler_params=pltpu.CompilerParams(vmem_limit_bytes=VMEM_BYTES),
        name="project",
    )(*operands)


def feed_kernel(state_ref, down_ref, up_ref, slope_ref, out_ref, acc_ref):
    step = pl.program_id(0)
    back = dot(state_ref[...], down_ref[...], NT)
    gated = (slope_ref[...] * back).astype(BF16)
    part = dot(gated, up_ref[...], NT)

    @pl.when(step == 0)
    def _():
        acc_ref[...] = part

    @pl.when(step > 0)
    def _():
        acc_ref[...] += part

    @pl.when(step == pl.num_programs(0) - 1)
    def _():
        out_ref[...] = acc_ref[...].astype(BF16)


def feed(state, down, up, slope):
    rows, width = state.shape
    hidden = up.shape[1]
    chunk = hidden if hidden % 128 else 128
    return pl.pallas_call(
        feed_kernel,
        grid=(hidden // chunk,),
        in_specs=[
            pl.BlockSpec((rows, width), lambda f: (0, 0)),
            pl.BlockSpec((chunk, width), lambda f: (f, 0)),
            pl.BlockSpec((width, chunk), lambda f: (0, f)),
            pl.BlockSpec((rows, chunk), lambda f: (0, f)),
        ],
        out_specs=pl.BlockSpec((rows, width), lambda f: (0, 0)),
        out_shape=jax.ShapeDtypeStruct((rows, width), BF16),
        scratch_shapes=[pltpu.VMEM((rows, width), F32)],
        compiler_params=pltpu.CompilerParams(vmem_limit_bytes=VMEM_BYTES),
        name="feed",
    )(state, down, up, slope)


def local(queries, keys, values, out_grad, key_proj, value_proj, global_in, up_proj, down_proj):
    size, planes = lax.axis_size("seq"), lax.axis_size("heads")
    place = lax.axis_index("seq") ^ jnp.arange(size, dtype=jnp.int32)
    chunk = lax.axis_index("heads") ^ jnp.arange(planes, dtype=jnp.int32)
    local_heads = queries.shape[1] // HD
    far = size // 2

    part = up_proj.shape[1] // planes
    up_parts = [
        lax.dynamic_slice_in_dim(up_proj, chunk[k] * part, part, 1) for k in range(planes)
    ]
    up_own = jnp.concatenate(
        [up_parts[0]] + [swap(up_parts[k], "heads", k) for k in range(1, planes)], 0
    )
    up = jnp.concatenate([up_own, swap(up_own, "seq", 1)], 1)
    down_parts = [
        lax.dynamic_slice_in_dim(down_proj, chunk[k] * part, part, 0) for k in range(planes)
    ]
    down_own = jnp.concatenate(
        [down_parts[0]] + [swap(down_parts[k], "heads", k) for k in range(1, planes)], 1
    )
    down = jnp.concatenate([down_own, swap(down_own, "seq", 1)], 0)
    wide_in = jnp.concatenate(gather_blocks(global_in, "heads", 1, planes), 1)
    all_in = jnp.concatenate(gather_blocks(wide_in, "seq", 2, far), 0)
    slope = slope_of(jnp.dot(all_in, up, preferred_element_type=F32))

    split = local_heads - 1
    query_grad, even, odd = attend(place, queries, out_grad, keys, values, None, 0, split)
    terms = scatter_rows(even, odd)
    query_grad, even, odd = attend(
        place, queries, out_grad, keys, values, query_grad, split, local_heads - split
    )
    first_share = project(chunk, terms, key_proj, value_proj, 0, None)
    share = project(chunk, scatter_rows(even, odd), key_proj, value_proj, split, first_share)
    state = share[0] + sum(
        swap(share[k].astype(BF16), "heads", k).astype(F32) for k in range(1, planes)
    )
    wide_state = jnp.concatenate(gather_blocks(state.astype(BF16), "heads", 1, planes), 1)
    all_state = jnp.concatenate(gather_blocks(wide_state, "seq", 2, far), 0)

    rows = state.shape[0]
    width = state.shape[1]
    grown = feed(all_state, down, up, slope)
    own_terms = scatter_terms(list(grown.reshape(far, rows, planes * width)), "seq", 2)
    own = sum(t.astype(F32) for t in own_terms)
    blocks = [own[:, k * width : (k + 1) * width] for k in range(planes)]
    global_grad = state + blocks[0] + sum(
        swap(blocks[k].astype(BF16), "heads", k).astype(F32) for k in range(1, planes)
    )
    return (query_grad, global_grad)


def solution(mesh):
    placed = (
        P("seq", "heads"),
        P(None, "heads"),
        P(None, "heads"),
        P("seq", "heads"),
        P(None, "heads"),
        P(None, "heads"),
        P("seq", "heads"),
        P("heads", "seq"),
        P("seq", "heads"),
    )
    return jax.shard_map(
        local,
        mesh=mesh,
        in_specs=placed,
        out_specs=(P("seq", "heads"), P("seq", "heads")),
        check_vma=False,
    )
```

```python
import functools
import math

import jax
import jax.numpy as jnp
from jax import lax
from jax.experimental import pallas as pl
from jax.experimental.pallas import tpu as pltpu
from jax.sharding import PartitionSpec as P

HD = 128
SCALE = HD**-0.5
SCALE_LOG2 = SCALE * math.log2(math.e)
BF16, F32 = jnp.bfloat16, jnp.float32
NT = (((1,), (1,)), ((), ()))
NN = (((1,), (0,)), ((), ()))
TN = (((0,), (0,)), ((), ()))
VMEM_BYTES = 48 * 2**20


def dot(a, b, dims):
    return lax.dot_general(a, b, dims, preferred_element_type=F32)


def slope_of(pre):
    return (
        0.5 * (1.0 + lax.erf(pre * 0.7071067811865476))
        + pre * jnp.exp(-0.5 * pre * pre) * 0.3989422804014327
    )


def swap(x, axis, distance):
    size = lax.axis_size(axis)
    return lax.ppermute(x, axis, [(i, i ^ distance) for i in range(size)])


def levels_of(first, count):
    levels = []
    while count > 1:
        radix = min(4, count)
        levels.append((first, radix))
        first, count = first * radix, count // radix
    return levels


def gather_blocks(x, axis, first, count):
    blocks = [x]
    for step, radix in levels_of(first, count):
        whole = blocks[0] if len(blocks) == 1 else jnp.stack(blocks)
        got = [swap(whole, axis, step * k) for k in range(1, radix)]
        for other in got:
            blocks = blocks + ([other] if whole is x else list(other))
    return blocks


def scatter_terms(blocks, axis, first, low=BF16):
    levels = levels_of(first, len(blocks))
    for step, radix in reversed(levels[1:]):
        span = step // first
        terms = [blocks[k * span : (k + 1) * span] for k in range(radix)]
        got = [swap(jnp.stack(terms[k]), axis, step * k) for k in range(1, radix)]
        blocks = [
            (terms[0][i].astype(F32) + sum(g[i].astype(F32) for g in got)).astype(low)
            for i in range(span)
        ]
    return [blocks[0]] + [swap(blocks[k], axis, first * k) for k in range(1, len(blocks))]


def attend_kernel(sub, place_ref, q_ref, g_ref, k_ref, v_ref, dq_ref, even_ref, odd_ref, acc_ref):
    block = pl.program_id(1)
    keys, values = k_ref[...], v_ref[...]

    @pl.when(block == 0)
    def _():
        acc_ref[...] = jnp.zeros_like(acc_ref)

    def products(at):
        return dot(keys, q_ref[at, :], NT), dot(values, g_ref[at, :], NT)

    def soften(scores, weight_grad):
        top = jnp.max(scores, axis=0, keepdims=True)
        grown = jnp.exp2((scores - top) * SCALE_LOG2)
        weights = grown * (1.0 / jnp.sum(grown, axis=0, keepdims=True))
        centre = jnp.sum(weights * weight_grad, axis=0, keepdims=True)
        return (weights * (weight_grad - centre)).astype(BF16), weights.astype(BF16)

    def collect(at, score_grad, weights_low):
        dq_ref[at, :] = (SCALE * dot(keys, score_grad, TN)).T.astype(BF16)
        acc_ref[:, :HD] += dot(score_grad, q_ref[at, :], NN)
        acc_ref[:, HD:] += dot(weights_low, g_ref[at, :], NN)

    pieces = [pl.ds(i * sub, sub) for i in range(q_ref.shape[0] // sub)]
    ahead, behind = products(pieces[0]), None
    for i, at in enumerate(pieces):
        now, ahead = ahead, products(pieces[i + 1]) if i + 1 < len(pieces) else None
        done = soften(*now)
        if behind is not None:
            collect(pieces[i - 1], *behind)
        behind = done
    collect(pieces[-1], *behind)

    @pl.when(block == pl.num_programs(1) - 1)
    def _():
        acc_ref[:, :HD] = SCALE * acc_ref[:, :HD]
        half, height = even_ref.shape[:2]
        for j in range(2 * half):
            at = pl.ds(pl.multiple_of(place_ref[j] * height, height), height)
            (odd_ref if j % 2 else even_ref)[j // 2] = acc_ref[at, :].astype(BF16)


def attend(place, queries, out_grad, keys, values):
    tokens, width = queries.shape
    glob, size, count = keys.shape[0], place.shape[0], width // HD
    block = min(2048, tokens)
    token_spec = pl.BlockSpec((block, HD), lambda h, b, place: (b, h))
    global_spec = pl.BlockSpec((glob, HD), lambda h, b, place: (0, h))
    part_spec = pl.BlockSpec((size // 2, glob // size, 2 * HD), lambda h, b, place: (0, 0, h))
    part = jax.ShapeDtypeStruct((size // 2, glob // size, 2 * width), BF16)
    return pl.pallas_call(
        functools.partial(attend_kernel, min(256, block)),
        grid_spec=pltpu.PrefetchScalarGridSpec(
            num_scalar_prefetch=1,
            grid=(count, tokens // block),
            in_specs=[token_spec, token_spec, global_spec, global_spec],
            out_specs=[token_spec, part_spec, part_spec],
            scratch_shapes=[pltpu.VMEM((glob, 2 * HD), F32)],
        ),
        out_shape=[jax.ShapeDtypeStruct((tokens, width), BF16), part, part],
        compiler_params=pltpu.CompilerParams(vmem_limit_bytes=60 * 2**20),
        cost_estimate=pl.CostEstimate(
            flops=20 * tokens * glob * width,
            bytes_accessed=6 * tokens * width,
            transcendentals=tokens * glob * count,
        ),
        name="attend",
    )(place, queries, out_grad, keys, values)


def merge_kernel(even_ref, got_ref, *out_refs):
    for j, out_ref in enumerate(out_refs):
        out_ref[...] = (even_ref[j].astype(F32) + got_ref[j].astype(F32)).astype(BF16)


def scatter_rows(even, odd):
    part = jax.ShapeDtypeStruct(even.shape[1:], BF16)
    mine = pl.pallas_call(
        merge_kernel,
        out_shape=[part] * even.shape[0],
        compiler_params=pltpu.CompilerParams(vmem_limit_bytes=VMEM_BYTES),
        cost_estimate=pl.CostEstimate(flops=even.size, bytes_accessed=6 * even.size, transcendentals=0),
        name="merge",
    )(even, swap(odd, "seq", 1))
    return scatter_terms(mine, "seq", 2)


def project_kernel(count, chunk_ref, *refs):
    terms = refs[:count]
    key_proj_ref, value_proj_ref, mixed_ref, part_ref, last_ref = refs[count:]
    total = sum(t[...].astype(F32) for t in terms).astype(BF16)
    heads = total.shape[1] // (2 * HD)
    pick = lambda at: [total[:, (2 * h + at) * HD : (2 * h + at + 1) * HD] for h in range(heads)]
    key_low, value_low = jnp.concatenate(pick(0), 1), jnp.concatenate(pick(1), 1)
    part = dot(key_low, key_proj_ref[...], NT) + dot(value_low, value_proj_ref[...], NT)
    part_ref[...] = part.astype(BF16)

    @pl.when(pl.program_id(0) == 0)
    def _():
        last_ref[...] = mixed_ref[...]


def project(chunk, terms, key_proj, value_proj, mixed):
    rows, width = terms[0].shape
    size = chunk.shape[0]
    block = key_proj.shape[0] // size
    last = mixed.shape[1] // rows - 1
    weight_spec = pl.BlockSpec((block, width // 2), lambda k, chunk: (chunk[k], 0))
    return pl.pallas_call(
        functools.partial(project_kernel, len(terms)),
        grid_spec=pltpu.PrefetchScalarGridSpec(
            num_scalar_prefetch=1,
            grid=(size,),
            in_specs=[pl.BlockSpec((rows, width), lambda k, chunk: (0, 0))] * len(terms)
            + [weight_spec] * 2
            + [pl.BlockSpec((size, rows, block), lambda k, chunk: (0, last, 0))],
            out_specs=[
                pl.BlockSpec((None, rows, block), lambda k, chunk: (k, 0, 0)),
                pl.BlockSpec((size, rows, block), lambda k, chunk: (0, 0, 0)),
            ],
        ),
        out_shape=[jax.ShapeDtypeStruct((size, rows, block), BF16)] * 2,
        compiler_params=pltpu.CompilerParams(vmem_limit_bytes=60 * 2**20),
        cost_estimate=pl.CostEstimate(
            flops=2 * rows * width * block * size,
            bytes_accessed=2 * width * block * size,
            transcendentals=0,
        ),
        name="project",
    )(chunk, *terms, key_proj, value_proj, mixed)


def back_kernel(count, chunk_ref, *refs):
    states, downs, out_ref = refs[:count], refs[count : count + 2], refs[-1]
    halves, size, rows, hidden = out_ref.shape
    height, hidden = states[0].shape[0] // halves, hidden // 2
    state = jnp.concatenate(
        [ref[c * height : (c + 1) * height, :] for c in range(halves) for ref in states], 0
    )
    for k in range(size):
        at = pl.ds(pl.multiple_of(chunk_ref[k] * hidden, hidden), hidden)
        for i in range(2):
            part = dot(state, downs[i][at, :], NT).astype(BF16)
            for c in range(halves):
                out_ref[c, k, :, i * hidden : (i + 1) * hidden] = part[c * rows : (c + 1) * rows]


def back_parts(chunk, states, downs, halves):
    size, (height, width) = chunk.shape[0], states[0].shape
    rows = len(states) * height
    if height % 16:
        states = [jnp.concatenate(states, 0)]
    hidden = downs[0].shape[0] // size
    return pl.pallas_call(
        functools.partial(back_kernel, len(states)),
        in_specs=[pl.BlockSpec(memory_space=pltpu.SMEM)]
        + [pl.BlockSpec(memory_space=pltpu.VMEM)] * (len(states) + 2),
        out_specs=pl.BlockSpec(memory_space=pltpu.VMEM),
        out_shape=jax.ShapeDtypeStruct((halves, size, rows // halves, 2 * hidden), BF16),
        compiler_params=pltpu.CompilerParams(vmem_limit_bytes=VMEM_BYTES),
        cost_estimate=pl.CostEstimate(
            flops=4 * rows * width * hidden * size,
            bytes_accessed=4 * width * hidden * size,
            transcendentals=0,
        ),
        name="back",
    )(chunk, *states, *downs)


def pre_kernel(count, *refs):
    inputs, ups, out_ref = refs[:count], refs[count : count + 2], refs[-1]
    halves, rows, hidden = out_ref.shape
    height, hidden = inputs[0].shape[1] // halves, hidden // 2
    size = ups[0].shape[0]
    whole = [
        jnp.concatenate(
            [ref[k, c * height : (c + 1) * height, :] for c in range(halves) for ref in inputs], 0
        )
        for k in range(size)
    ]
    for i in range(2):
        part = sum(dot(whole[k], ups[i][k, :hidden, :], NT) for k in range(size))
        for c in range(halves):
            out_ref[c, :, i * hidden : (i + 1) * hidden] = part[c * rows : (c + 1) * rows]


def pre_parts(inputs, ups, hidden, halves):
    height = inputs[0].shape[1]
    rows = len(inputs) * height // halves
    if height % 16:
        inputs = [jnp.concatenate(inputs, 1)]
    return pl.pallas_call(
        functools.partial(pre_kernel, len(inputs)),
        out_shape=jax.ShapeDtypeStruct((halves, rows, 2 * hidden), F32),
        compiler_params=pltpu.CompilerParams(vmem_limit_bytes=VMEM_BYTES),
        cost_estimate=pl.CostEstimate(
            flops=4 * halves * rows * hidden * ups[0].shape[0] * ups[0].shape[2],
            bytes_accessed=4 * ups[0].size,
            transcendentals=0,
        ),
        name="pre",
    )(*inputs, *ups)


def feed_kernel(count, chunk_ref, *refs):
    terms, slope_ref, ups, out_ref = refs[:count], refs[count], refs[count + 1 : count + 3], refs[-1]
    back = sum(ref[...].astype(F32) for ref in terms)
    gated = (slope_ref[...] * back).astype(BF16)
    hidden = gated.shape[1] // 2
    size, _, width = ups[0].shape
    for k in range(size):
        part = sum(
            dot(gated[:, i * hidden : (i + 1) * hidden], ups[i][chunk_ref[k], :hidden, :], NN)
            for i in range(2)
        )
        out_ref[:, :, k * width : (k + 1) * width] = part.astype(BF16).reshape(
            out_ref.shape[0], out_ref.shape[1], width
        )


def feed(chunk, terms, slope, ups, blocks):
    rows = terms[0].shape[0]
    size, _, width = ups[0].shape
    hidden = terms[0].shape[1] // 2
    return pl.pallas_call(
        functools.partial(feed_kernel, len(terms)),
        in_specs=[pl.BlockSpec(memory_space=pltpu.SMEM)]
        + [pl.BlockSpec(memory_space=pltpu.VMEM)] * (len(terms) + 3),
        out_specs=pl.BlockSpec(memory_space=pltpu.VMEM),
        out_shape=jax.ShapeDtypeStruct((blocks, rows // blocks, size * width), BF16),
        compiler_params=pltpu.CompilerParams(vmem_limit_bytes=VMEM_BYTES),
        cost_estimate=pl.CostEstimate(
            flops=4 * rows * hidden * width * size,
            bytes_accessed=4 * hidden * width * size,
            transcendentals=0,
        ),
        name="feed",
    )(chunk, *terms, slope, *ups)


def local(queries, keys, values, out_grad, key_proj, value_proj, global_in, up_proj, down_proj):
    size, planes = lax.axis_size("seq"), lax.axis_size("heads")
    place = lax.axis_index("seq") ^ jnp.arange(size, dtype=jnp.int32)
    chunk = lax.axis_index("heads") ^ jnp.arange(planes, dtype=jnp.int32)
    far = size // 2
    rows, width = global_in.shape
    halves = 2 if rows % 32 == 0 else 1

    own_up = up_proj.T.reshape(planes, -1, width)
    hidden = own_up.shape[1]
    sent = jnp.broadcast_to(global_in[None], (planes, rows, width))
    own_up = lax.all_to_all(jnp.concatenate([own_up, sent], 1), "heads", 0, 0)
    downs = [down_proj, swap(down_proj, "seq", 1)]

    query_grad, even, odd = attend(place, queries, out_grad, keys, values)
    share, input_part = project(chunk, scatter_rows(even, odd), key_proj, value_proj, own_up)
    late_up, share = lax.optimization_barrier((own_up, share))
    ups = [own_up, swap(late_up, "seq", 1)]
    state = sum(
        t.astype(F32) for t in [share[0]] + [swap(share[k], "heads", k) for k in range(1, planes)]
    )
    inputs = gather_blocks(input_part, "seq", 2, far)
    states = gather_blocks(state.astype(BF16), "seq", 2, far)
    parts = back_parts(chunk, states, downs, halves)
    slope = slope_of(pre_parts(inputs, ups, hidden, halves))

    terms = [
        [parts[c, 0]] + [swap(parts[c, k], "heads", k) for k in range(1, planes)]
        for c in range(halves)
    ]
    grown = [feed(chunk, terms[c], slope[c], ups, far) for c in range(halves)]
    own_terms = [scatter_terms([g[j] for j in range(far)], "seq", 2) for g in grown]
    grads = []
    for c in range(halves):
        own = sum(t.astype(F32) for t in own_terms[c])
        blocks = [own[:, k * width : (k + 1) * width] for k in range(planes)]
        grads.append(
            blocks[0]
            + sum(swap(blocks[k].astype(BF16), "heads", k).astype(F32) for k in range(1, planes))
        )
    global_grad = state + jnp.concatenate(grads, 0)
    return (query_grad, global_grad)


def solution(mesh):
    placed = (
        P("seq", "heads"),
        P(None, "heads"),
        P(None, "heads"),
        P("seq", "heads"),
        P(None, "heads"),
        P(None, "heads"),
        P("seq", "heads"),
        P("heads", "seq"),
        P("seq", "heads"),
    )
    return jax.shard_map(
        local,
        mesh=mesh,
        in_specs=placed,
        out_specs=(P("seq", "heads"), P("seq", "heads")),
        check_vma=False,
    )
```

```python
import functools
import math

import jax
import jax.numpy as jnp
from jax import lax
from jax.experimental import pallas as pl
from jax.experimental.pallas import tpu as pltpu
from jax.sharding import PartitionSpec as P

HD = 128
SCALE = HD**-0.5
SCALE_LOG2 = SCALE * math.log2(math.e)
BF16, F32 = jnp.bfloat16, jnp.float32
NT = (((1,), (1,)), ((), ()))
NN = (((1,), (0,)), ((), ()))
TN = (((0,), (0,)), ((), ()))
VMEM_BYTES = 24 * 2**20


def dot(a, b, dims):
    return lax.dot_general(a, b, dims, preferred_element_type=F32)


def slope_of(pre):
    return (
        0.5 * (1.0 + lax.erf(pre * 0.7071067811865476))
        + pre * jnp.exp(-0.5 * pre * pre) * 0.3989422804014327
    )


def swap(x, axis, distance):
    size = lax.axis_size(axis)
    return lax.ppermute(x, axis, [(i, i ^ distance) for i in range(size)])


def levels_of(first, count):
    levels = []
    while count > 1:
        radix = min(4, count)
        levels.append((first, radix))
        first, count = first * radix, count // radix
    return levels


def gather_blocks(x, axis, first, count):
    blocks = [x]
    for step, radix in levels_of(first, count):
        whole = blocks[0] if len(blocks) == 1 else jnp.stack(blocks)
        got = [swap(whole, axis, step * k) for k in range(1, radix)]
        for other in got:
            blocks = blocks + ([other] if whole is x else list(other))
    return blocks


def scatter_terms(blocks, axis, first, low=BF16):
    levels = levels_of(first, len(blocks))
    for step, radix in reversed(levels[1:]):
        span = step // first
        terms = [blocks[k * span : (k + 1) * span] for k in range(radix)]
        got = [swap(jnp.stack(terms[k]), axis, step * k) for k in range(1, radix)]
        blocks = [
            (terms[0][i].astype(F32) + sum(g[i].astype(F32) for g in got)).astype(low)
            for i in range(span)
        ]
    return [blocks[0]] + [swap(blocks[k], axis, first * k) for k in range(1, len(blocks))]


def attend_kernel(sub, place_ref, q_ref, g_ref, k_ref, v_ref, *rest):
    dq_ref, even_ref, odd_ref, acc_ref = rest[-4:]
    block = pl.program_id(1)
    keys, values = k_ref[...], v_ref[...]

    @pl.when(block == 0)
    def _():
        acc_ref[...] = jnp.zeros_like(acc_ref)

    def products(at):
        return dot(keys, q_ref[at, :], NT), dot(values, g_ref[at, :], NT)

    def soften(scores, weight_grad):
        top = jnp.max(scores, axis=0, keepdims=True)
        grown = jnp.exp2((scores - top) * SCALE_LOG2)
        weights = grown * (1.0 / jnp.sum(grown, axis=0, keepdims=True))
        centre = jnp.sum(weights * weight_grad, axis=0, keepdims=True)
        return (weights * (weight_grad - centre)).astype(BF16), weights.astype(BF16)

    def collect(at, score_grad, weights_low):
        dq_ref[at, :] = (SCALE * dot(keys, score_grad, TN)).T.astype(BF16)
        acc_ref[:, :HD] += dot(score_grad, q_ref[at, :], NN)
        acc_ref[:, HD:] += dot(weights_low, g_ref[at, :], NN)

    pieces = [pl.ds(i * sub, sub) for i in range(q_ref.shape[0] // sub)]
    ahead, behind = products(pieces[0]), None
    for i, at in enumerate(pieces):
        now, ahead = ahead, products(pieces[i + 1]) if i + 1 < len(pieces) else None
        done = soften(*now)
        if behind is not None:
            collect(pieces[i - 1], *behind)
        behind = done
    collect(pieces[-1], *behind)

    @pl.when(block == pl.num_programs(1) - 1)
    def _():
        acc_ref[:, :HD] = SCALE * acc_ref[:, :HD]
        half, height = even_ref.shape[:2]
        for j in range(2 * half):
            at = pl.ds(pl.multiple_of(place_ref[j] * height, height), height)
            (odd_ref if j % 2 else even_ref)[j // 2] = acc_ref[at, :].astype(BF16)


def attend(place, queries, out_grad, keys, values, first, count, query_grad=None, after=()):
    tokens, width = queries.shape
    glob, size = keys.shape[0], place.shape[0]
    block = min(2048, tokens)
    token_spec = pl.BlockSpec((block, HD), lambda h, b, place: (b, h + first))
    global_spec = pl.BlockSpec((glob, HD), lambda h, b, place: (0, h + first))
    part_spec = pl.BlockSpec((size // 2, glob // size, 2 * HD), lambda h, b, place: (0, 0, h))
    part = pltpu.HBM((size // 2, glob // size, 2 * HD * count), BF16)
    extra = [x for x in (query_grad, *after) if x is not None]
    return pl.pallas_call(
        functools.partial(attend_kernel, min(256, block)),
        grid_spec=pltpu.PrefetchScalarGridSpec(
            num_scalar_prefetch=1,
            grid=(count, tokens // block),
            in_specs=[token_spec, token_spec, global_spec, global_spec]
            + [pl.BlockSpec(memory_space=pl.ANY)] * len(extra),
            out_specs=[token_spec, part_spec, part_spec],
            scratch_shapes=[pltpu.VMEM((glob, 2 * HD), F32)],
        ),
        out_shape=[pltpu.HBM((tokens, width), BF16), part, part],
        input_output_aliases={} if query_grad is None else {5: 0},
        compiler_params=pltpu.CompilerParams(vmem_limit_bytes=VMEM_BYTES),
        cost_estimate=pl.CostEstimate(
            flops=20 * tokens * glob * HD * count,
            bytes_accessed=6 * tokens * HD * count,
            transcendentals=tokens * glob * count,
        ),
        name="attend",
    )(place, *map(hold, (queries, out_grad, keys, values)), *extra)


def hold(x):
    return pltpu.with_memory_space_constraint(x, pltpu.HBM)


def bundle_kernel(up_ref, in_ref, out_ref):
    size, depth, _ = out_ref.shape
    rows = in_ref.shape[0]
    hidden = depth - rows
    for k in range(size):
        out_ref[k, :hidden, :] = up_ref[:, k * hidden : (k + 1) * hidden].T
        out_ref[k, hidden:, :] = in_ref[...]


def bundle(up_proj, global_in, size):
    (width, hidden), rows = up_proj.shape, global_in.shape[0]
    if (hidden // size) % 128 or rows % 16:
        return jnp.concatenate(
            [
                up_proj.T.reshape(size, hidden // size, width),
                jnp.broadcast_to(global_in[None], (size, rows, width)),
            ],
            1,
        )
    return pl.pallas_call(
        bundle_kernel,
        out_shape=jax.ShapeDtypeStruct((size, hidden // size + rows, width), BF16),
        compiler_params=pltpu.CompilerParams(vmem_limit_bytes=VMEM_BYTES),
        cost_estimate=pl.CostEstimate(
            flops=0, bytes_accessed=4 * up_proj.size, transcendentals=0
        ),
        name="bundle",
    )(hold(up_proj), hold(global_in))


def merge_kernel(count, *refs):
    evens, gots = refs[:count], refs[count : 2 * count]
    out_refs = refs[len(refs) - evens[0].shape[0] :]
    at = 0
    for even_ref, got_ref in zip(evens, gots):
        cols = pl.ds(at, even_ref.shape[2])
        at += even_ref.shape[2]
        for j, out_ref in enumerate(out_refs):
            out_ref[:, cols] = (even_ref[j].astype(F32) + got_ref[j].astype(F32)).astype(BF16)


def scatter_rows(evens, odds, near):
    gots = [swap(odd, "seq", 1) for odd in odds]
    blocks, rows, _ = evens[0].shape
    width = sum(even.shape[2] for even in evens)
    spec = lambda x: pl.BlockSpec(x.shape, lambda: (0, 0, 0))
    mine = pl.pallas_call(
        functools.partial(merge_kernel, len(evens)),
        in_specs=[spec(x) for x in (*evens, *gots)]
        + [pl.BlockSpec(memory_space=pltpu.VMEM)] * len(near),
        out_shape=[jax.ShapeDtypeStruct((rows, width), BF16)] * blocks,
        compiler_params=pltpu.CompilerParams(vmem_limit_bytes=VMEM_BYTES),
        cost_estimate=pl.CostEstimate(
            flops=blocks * rows * width, bytes_accessed=6 * blocks * rows * width, transcendentals=0
        ),
        name="merge",
    )(*map(hold, evens), *gots, *near)
    return scatter_terms(mine, "seq", 2)


def project_kernel(count, chunk_ref, *refs):
    terms, sources = refs[:count], refs[count : count + 2]
    part_refs, (term_ref, held_ref, term_sems, sems) = refs[count + 2 : -4], refs[-4:]
    size, block = len(part_refs), part_refs[0].shape[1]

    def fetch(k, i):
        at = pl.ds(pl.multiple_of(chunk_ref[k] * block, block), block)
        return pltpu.make_async_copy(sources[i].at[at, :], held_ref.at[k, i], sems.at[k, i])

    given = [pltpu.make_async_copy(t, term_ref.at[j], term_sems.at[j]) for j, t in enumerate(terms)]
    for copy in given:
        copy.start()
    for k in range(size):
        for i in range(2):
            fetch(k, i).start()
    for copy in given:
        copy.wait()
    total = sum(term_ref[j].astype(F32) for j in range(count)).astype(BF16)
    heads = total.shape[1] // (2 * HD)
    low = [
        jnp.concatenate([total[:, (2 * h + i) * HD : (2 * h + i + 1) * HD] for h in range(heads)], 1)
        for i in range(2)
    ]
    for k, part_ref in enumerate(part_refs):
        part = None
        for i in range(2):
            fetch(k, i).wait()
            term = dot(low[i], held_ref[k, i], NT)
            part = term if part is None else part + term
        part_ref[...] = part.astype(BF16)


def project(chunk, terms, key_proj, value_proj):
    rows, width = terms[0].shape
    size = chunk.shape[0]
    block = key_proj.shape[0] // size
    count = len(terms)
    part = pltpu.HBM((rows, block), BF16)
    return pl.pallas_call(
        functools.partial(project_kernel, count),
        in_specs=[pl.BlockSpec(memory_space=pltpu.SMEM)]
        + [pl.BlockSpec(memory_space=pl.ANY)] * (count + 2),
        out_specs=[pl.BlockSpec((rows, block), lambda: (0, 0))] * size,
        out_shape=[part] * size,
        scratch_shapes=[
            pltpu.VMEM((count, rows, width), BF16),
            pltpu.VMEM((size, 2, block, width // 2), BF16),
            pltpu.SemaphoreType.DMA((count,)),
            pltpu.SemaphoreType.DMA((size, 2)),
        ],
        compiler_params=pltpu.CompilerParams(vmem_limit_bytes=VMEM_BYTES),
        cost_estimate=pl.CostEstimate(
            flops=2 * rows * width * block * size,
            bytes_accessed=2 * width * block * size,
            transcendentals=0,
        ),
        name="project",
    )(chunk, *terms, hold(key_proj), hold(value_proj))


def pieces_of(blocks, cuts):
    height = sum(cuts)
    starts = [sum(cuts[:c]) for c in range(len(cuts))]
    whole = blocks[0].shape[0] // height
    rows = [
        block[i * height + start : i * height + start + cut]
        for start, cut in zip(starts, cuts)
        for block in blocks
        for i in range(whole)
    ]
    count = len(blocks) * whole
    return jnp.concatenate(rows, 0), [(count * start, count * cut) for start, cut in zip(starts, cuts)]


def back_kernel(count, cuts, chunk_ref, *refs):
    states, downs, out_refs = refs[:count], refs[count : count + 2], refs[count + 2 :]
    size, _, hidden = out_refs[0].shape
    hidden = hidden // 2
    state, places = pieces_of([ref[...] for ref in states], cuts)
    for k in range(size):
        at = pl.ds(pl.multiple_of(chunk_ref[k] * hidden, hidden), hidden)
        for i in range(2):
            part = dot(state, downs[i][at, :], NT).astype(BF16)
            for (start, rows), out_ref in zip(places, out_refs):
                out_ref[k, :, i * hidden : (i + 1) * hidden] = part[start : start + rows]


def back_parts(chunk, states, downs, cuts):
    size, (height, width) = chunk.shape[0], states[0].shape
    count = len(states)
    if height % 16:
        states = [jnp.concatenate(states, 0)]
    hidden = downs[0].shape[0] // size
    return pl.pallas_call(
        functools.partial(back_kernel, len(states), cuts),
        in_specs=[pl.BlockSpec(memory_space=pltpu.SMEM)]
        + [pl.BlockSpec(memory_space=pltpu.VMEM)] * (len(states) + 2),
        out_shape=[jax.ShapeDtypeStruct((size, count * cut, 2 * hidden), BF16) for cut in cuts],
        compiler_params=pltpu.CompilerParams(vmem_limit_bytes=VMEM_BYTES),
        cost_estimate=pl.CostEstimate(
            flops=4 * count * height * width * hidden * size,
            bytes_accessed=4 * width * hidden * size,
            transcendentals=0,
        ),
        name="back",
    )(chunk, *states, *downs)


def pre_kernel(count, cuts, *refs):
    inputs, ups, out_refs = refs[:count], refs[count : count + 2], refs[len(refs) - len(cuts) :]
    hidden = out_refs[0].shape[1] // 2
    size = ups[0].shape[0]
    whole = [pieces_of([ref[k] for ref in inputs], cuts) for k in range(size)]
    for i in range(2):
        part = sum(dot(whole[k][0], ups[i][k, :hidden, :], NT) for k in range(size))
        for (start, rows), out_ref in zip(whole[0][1], out_refs):
            out_ref[:, i * hidden : (i + 1) * hidden] = part[start : start + rows]


def pre_parts(inputs, ups, hidden, cuts, after):
    count, height = len(inputs), inputs[0].shape[1]
    if height % 16:
        inputs = [jnp.concatenate(inputs, 1)]
    return pl.pallas_call(
        functools.partial(pre_kernel, len(inputs), cuts),
        in_specs=[pl.BlockSpec(x.shape, lambda: (0, 0, 0)) for x in (*inputs, *ups)]
        + [pl.BlockSpec(memory_space=pl.ANY)] * len(after),
        out_shape=[jax.ShapeDtypeStruct((count * cut, 2 * hidden), F32) for cut in cuts],
        compiler_params=pltpu.CompilerParams(vmem_limit_bytes=VMEM_BYTES),
        cost_estimate=pl.CostEstimate(
            flops=4 * count * height * hidden * ups[0].shape[0] * ups[0].shape[2],
            bytes_accessed=4 * ups[0].size,
            transcendentals=0,
        ),
        name="pre",
    )(*inputs, *ups, *after)


def feed_kernel(count, chunk_ref, *refs):
    terms, slope_ref, ups, out_ref = refs[:count], refs[count], refs[count + 1 : count + 3], refs[-1]
    back = sum(ref[...].astype(F32) for ref in terms)
    gated = (slope_ref[...] * back).astype(BF16)
    hidden = gated.shape[1] // 2
    size, _, width = ups[0].shape
    for k in range(size):
        part = sum(
            dot(gated[:, i * hidden : (i + 1) * hidden], ups[i][chunk_ref[k], :hidden, :], NN)
            for i in range(2)
        )
        out_ref[:, :, k * width : (k + 1) * width] = part.astype(BF16).reshape(
            out_ref.shape[0], out_ref.shape[1], width
        )


def feed(chunk, terms, slope, ups, blocks):
    rows = terms[0].shape[0]
    size, _, width = ups[0].shape
    hidden = terms[0].shape[1] // 2
    return pl.pallas_call(
        functools.partial(feed_kernel, len(terms)),
        in_specs=[pl.BlockSpec(memory_space=pltpu.SMEM)]
        + [pl.BlockSpec(memory_space=pltpu.VMEM)] * (len(terms) + 3),
        out_specs=pl.BlockSpec(memory_space=pltpu.VMEM),
        out_shape=jax.ShapeDtypeStruct((blocks, rows // blocks, size * width), BF16),
        compiler_params=pltpu.CompilerParams(vmem_limit_bytes=VMEM_BYTES),
        cost_estimate=pl.CostEstimate(
            flops=4 * rows * hidden * width * size,
            bytes_accessed=4 * hidden * width * size,
            transcendentals=0,
        ),
        name="feed",
    )(chunk, *terms, slope, *ups)


def local(queries, keys, values, out_grad, key_proj, value_proj, global_in, up_proj, down_proj):
    size, planes = lax.axis_size("seq"), lax.axis_size("heads")
    place = lax.axis_index("seq") ^ jnp.arange(size, dtype=jnp.int32)
    chunk = lax.axis_index("heads") ^ jnp.arange(planes, dtype=jnp.int32)
    far = size // 2
    rows, width = global_in.shape
    cuts = (rows // 2, rows // 2) if rows % 32 == 0 else (rows,)

    downs = [down_proj, swap(down_proj, "seq", 1)]
    hidden = up_proj.shape[1] // planes
    own_up = lax.all_to_all(bundle(up_proj, global_in, planes), "heads", 0, 0)

    arrays = (queries, out_grad, keys, values)
    heads = queries.shape[1] // HD
    query_grad, even, odd = attend(place, *arrays, 0, heads)
    terms = scatter_rows([even], [odd], [])
    terms[0], downs[1] = lax.optimization_barrier((terms[0], downs[1]))
    share = list(project(chunk, terms, key_proj, value_proj))
    own_up, share[0] = lax.optimization_barrier((own_up, share[0]))
    ups = [own_up, swap(own_up, "seq", 1)]
    shares = [share[0]] + [swap(share[k], "heads", k) for k in range(1, planes)]
    shares, ups[1] = lax.optimization_barrier((shares, ups[1]))
    state = sum(t.astype(F32) for t in shares)
    state_low = state.astype(BF16)
    inputs = gather_blocks(own_up[:, hidden:], "seq", 2, far)
    states = gather_blocks(state_low, "seq", 2, far)
    parts = back_parts(chunk, states, downs, cuts)
    slopes = [slope_of(pre) for pre in pre_parts(inputs, ups, hidden, cuts, parts[:1])]

    grads = []
    for part, slope in zip(parts, slopes):
        terms = [part[0]] + [swap(part[k], "heads", k) for k in range(1, planes)]
        grown = feed(chunk, terms, slope, ups, far)
        own = sum(t.astype(F32) for t in scatter_terms([grown[j] for j in range(far)], "seq", 2))
        blocks = [own[:, k * width : (k + 1) * width] for k in range(planes)]
        grads.append(
            blocks[0]
            + sum(swap(blocks[k].astype(BF16), "heads", k).astype(F32) for k in range(1, planes))
        )
    global_grad = state + jnp.concatenate(grads, 0)
    return (query_grad, global_grad)


def solution(mesh):
    placed = (
        P("seq", "heads"),
        P(None, "heads"),
        P(None, "heads"),
        P("seq", "heads"),
        P(None, "heads"),
        P(None, "heads"),
        P("seq", "heads"),
        P("heads", "seq"),
        P("seq", "heads"),
    )
    return jax.shard_map(
        local,
        mesh=mesh,
        in_specs=placed,
        out_specs=(P("seq", "heads"), P("seq", "heads")),
        check_vma=False,
    )
```

```python
import functools
import math

import jax
import jax.numpy as jnp
from jax import lax
from jax.experimental import pallas as pl
from jax.experimental.pallas import tpu as pltpu
from jax.sharding import PartitionSpec as P

HD = 128
SCALE = HD**-0.5
SCALE_LOG2 = SCALE * math.log2(math.e)
BF16, F32 = jnp.bfloat16, jnp.float32
NT = (((1,), (1,)), ((), ()))
NN = (((1,), (0,)), ((), ()))
TN = (((0,), (0,)), ((), ()))
VMEM_BYTES = 24 * 2**20


def dot(a, b, dims):
    return lax.dot_general(a, b, dims, preferred_element_type=F32)


def slope_of(pre):
    return (
        0.5 * (1.0 + lax.erf(pre * 0.7071067811865476))
        + pre * jnp.exp(-0.5 * pre * pre) * 0.3989422804014327
    )


def swap(x, axis, distance):
    size = lax.axis_size(axis)
    return lax.ppermute(x, axis, [(i, i ^ distance) for i in range(size)])


def levels_of(first, count):
    levels = []
    while count > 1:
        radix = min(4, count)
        levels.append((first, radix))
        first, count = first * radix, count // radix
    return levels


def gather_blocks(x, axis, first, count):
    blocks = [x]
    for step, radix in levels_of(first, count):
        whole = blocks[0] if len(blocks) == 1 else jnp.stack(blocks)
        got = [swap(whole, axis, step * k) for k in range(1, radix)]
        for other in got:
            blocks = blocks + ([other] if whole is x else list(other))
    return blocks


def scatter_terms(blocks, axis, first, low=BF16):
    levels = levels_of(first, len(blocks))
    for step, radix in reversed(levels[1:]):
        span = step // first
        terms = [blocks[k * span : (k + 1) * span] for k in range(radix)]
        got = [swap(jnp.stack(terms[k]), axis, step * k) for k in range(1, radix)]
        blocks = [
            (terms[0][i].astype(F32) + sum(g[i].astype(F32) for g in got)).astype(low)
            for i in range(span)
        ]
    return [blocks[0]] + [swap(blocks[k], axis, first * k) for k in range(1, len(blocks))]


def attend_kernel(sub, place_ref, q_ref, g_ref, k_ref, v_ref, *rest):
    dq_ref, even_ref, odd_ref, acc_ref = rest[-4:]
    block = pl.program_id(1)
    keys, values = k_ref[...], v_ref[...]

    @pl.when(block == 0)
    def _():
        acc_ref[...] = jnp.zeros_like(acc_ref)

    def products(at):
        return dot(keys, q_ref[at, :], NT), dot(values, g_ref[at, :], NT)

    def soften(scores, weight_grad):
        top = jnp.max(scores, axis=0, keepdims=True)
        grown = jnp.exp2((scores - top) * SCALE_LOG2)
        weights = grown * (1.0 / jnp.sum(grown, axis=0, keepdims=True))
        centre = jnp.sum(weights * weight_grad, axis=0, keepdims=True)
        return (weights * (weight_grad - centre)).astype(BF16), weights.astype(BF16)

    def collect(at, score_grad, weights_low):
        dq_ref[at, :] = (SCALE * dot(keys, score_grad, TN)).T.astype(BF16)
        acc_ref[:, :HD] += dot(score_grad, q_ref[at, :], NN)
        acc_ref[:, HD:] += dot(weights_low, g_ref[at, :], NN)

    pieces = [pl.ds(i * sub, sub) for i in range(q_ref.shape[0] // sub)]
    ahead, behind = products(pieces[0]), None
    for i, at in enumerate(pieces):
        now, ahead = ahead, products(pieces[i + 1]) if i + 1 < len(pieces) else None
        done = soften(*now)
        if behind is not None:
            collect(pieces[i - 1], *behind)
        behind = done
    collect(pieces[-1], *behind)

    @pl.when(block == pl.num_programs(1) - 1)
    def _():
        acc_ref[:, :HD] = SCALE * acc_ref[:, :HD]
        half, height = even_ref.shape[:2]
        for j in range(2 * half):
            at = pl.ds(pl.multiple_of(place_ref[j] * height, height), height)
            (odd_ref if j % 2 else even_ref)[j // 2] = acc_ref[at, :].astype(BF16)


def attend(place, queries, out_grad, keys, values, first, count, query_grad=None, after=()):
    tokens, width = queries.shape
    glob, size = keys.shape[0], place.shape[0]
    block = min(2048, tokens)
    token_spec = pl.BlockSpec((block, HD), lambda h, b, place: (b, h + first))
    global_spec = pl.BlockSpec((glob, HD), lambda h, b, place: (0, h + first))
    part_spec = pl.BlockSpec((size // 2, glob // size, 2 * HD), lambda h, b, place: (0, 0, h))
    part = pltpu.VMEM((size // 2, glob // size, 2 * HD * count), BF16)
    extra = [x for x in (query_grad, *after) if x is not None]
    return pl.pallas_call(
        functools.partial(attend_kernel, min(256, block)),
        grid_spec=pltpu.PrefetchScalarGridSpec(
            num_scalar_prefetch=1,
            grid=(count, tokens // block),
            in_specs=[token_spec, token_spec, global_spec, global_spec]
            + [pl.BlockSpec(memory_space=pl.ANY)] * len(extra),
            out_specs=[token_spec, part_spec, part_spec],
            scratch_shapes=[pltpu.VMEM((glob, 2 * HD), F32)],
        ),
        out_shape=[pltpu.HBM((tokens, width), BF16), part, part],
        input_output_aliases={} if query_grad is None else {5: 0},
        compiler_params=pltpu.CompilerParams(vmem_limit_bytes=VMEM_BYTES),
        cost_estimate=pl.CostEstimate(
            flops=20 * tokens * glob * HD * count,
            bytes_accessed=6 * tokens * HD * count,
            transcendentals=tokens * glob * count,
        ),
        name="attend",
    )(place, *map(hold, (queries, out_grad, keys, values)), *extra)


def hold(x):
    return pltpu.with_memory_space_constraint(x, pltpu.HBM)


def bundle_kernel(up_ref, in_ref, out_ref):
    size, depth, _ = out_ref.shape
    rows = in_ref.shape[0]
    hidden = depth - rows
    for k in range(size):
        out_ref[k, :hidden, :] = up_ref[:, k * hidden : (k + 1) * hidden].T
        out_ref[k, hidden:, :] = in_ref[...]


def bundle(up_proj, global_in, size):
    (width, hidden), rows = up_proj.shape, global_in.shape[0]
    if (hidden // size) % 128 or rows % 16:
        return jnp.concatenate(
            [
                up_proj.T.reshape(size, hidden // size, width),
                jnp.broadcast_to(global_in[None], (size, rows, width)),
            ],
            1,
        )
    return pl.pallas_call(
        bundle_kernel,
        out_shape=jax.ShapeDtypeStruct((size, hidden // size + rows, width), BF16),
        compiler_params=pltpu.CompilerParams(vmem_limit_bytes=VMEM_BYTES),
        cost_estimate=pl.CostEstimate(
            flops=0, bytes_accessed=4 * up_proj.size, transcendentals=0
        ),
        name="bundle",
    )(hold(up_proj), hold(global_in))


def merge_kernel(count, *refs):
    evens, gots = refs[:count], refs[count : 2 * count]
    out_refs = refs[len(refs) - evens[0].shape[0] :]
    at = 0
    for even_ref, got_ref in zip(evens, gots):
        cols = pl.ds(at, even_ref.shape[2])
        at += even_ref.shape[2]
        for j, out_ref in enumerate(out_refs):
            out_ref[:, cols] = (even_ref[j].astype(F32) + got_ref[j].astype(F32)).astype(BF16)


def scatter_rows(evens, odds, near):
    gots = [swap(odd, "seq", 1) for odd in odds]
    blocks, rows, _ = evens[0].shape
    width = sum(even.shape[2] for even in evens)
    spec = lambda x: pl.BlockSpec(x.shape, lambda: (0, 0, 0))
    mine = pl.pallas_call(
        functools.partial(merge_kernel, len(evens)),
        in_specs=[spec(x) for x in (*evens, *gots)]
        + [pl.BlockSpec(memory_space=pltpu.VMEM)] * len(near),
        out_shape=[pltpu.VMEM((rows, width), BF16)] * blocks,
        compiler_params=pltpu.CompilerParams(vmem_limit_bytes=VMEM_BYTES),
        cost_estimate=pl.CostEstimate(
            flops=blocks * rows * width, bytes_accessed=6 * blocks * rows * width, transcendentals=0
        ),
        name="merge",
    )(*evens, *gots, *near)
    return scatter_terms(mine, "seq", 2)


def prepare_kernel(*refs):
    half = len(refs) // 2
    for from_ref, to_ref in zip(refs[:half], refs[half:]):
        to_ref[...] = from_ref[...]


def prepare(arrays, after):
    count = len(arrays)
    return pl.pallas_call(
        lambda *refs: prepare_kernel(*refs[:count], *refs[count + len(after) :]),
        grid=(4,),
        in_specs=[pl.BlockSpec((x.shape[0] // 4, x.shape[1]), lambda i: (i, 0)) for x in arrays]
        + [pl.BlockSpec(memory_space=pl.ANY)] * len(after),
        out_specs=[pl.BlockSpec((x.shape[0] // 4, x.shape[1]), lambda i: (i, 0)) for x in arrays],
        out_shape=[pltpu.VMEM(x.shape, x.dtype) for x in arrays],
        compiler_params=pltpu.CompilerParams(vmem_limit_bytes=VMEM_BYTES),
        cost_estimate=pl.CostEstimate(
            flops=0, bytes_accessed=4 * sum(x.size for x in arrays), transcendentals=0
        ),
        name="prepare",
    )(*map(hold, arrays), *after)


def project_kernel(count, chunk_ref, *refs):
    terms, (key_proj_ref, value_proj_ref) = refs[:count], refs[count : count + 2]
    part_refs = refs[count + 2 :]
    total = sum(t[...].astype(F32) for t in terms).astype(BF16)
    heads = total.shape[1] // (2 * HD)
    pick = lambda at: [total[:, (2 * h + at) * HD : (2 * h + at + 1) * HD] for h in range(heads)]
    key_low, value_low = jnp.concatenate(pick(0), 1), jnp.concatenate(pick(1), 1)
    block = part_refs[0].shape[1]
    for k, part_ref in enumerate(part_refs):
        at = pl.ds(pl.multiple_of(chunk_ref[k] * block, block), block)
        part = dot(key_proj_ref[at, :], key_low, NT) + dot(value_proj_ref[at, :], value_low, NT)
        part_ref[...] = part.T.astype(BF16)


def project(chunk, terms, key_proj, value_proj):
    rows, width = terms[0].shape
    size = chunk.shape[0]
    block = key_proj.shape[0] // size
    part = pltpu.HBM((rows, block), BF16)
    return pl.pallas_call(
        functools.partial(project_kernel, len(terms)),
        in_specs=[pl.BlockSpec(memory_space=pltpu.SMEM)]
        + [pl.BlockSpec(memory_space=pltpu.VMEM)] * (len(terms) + 2),
        out_specs=[pl.BlockSpec((rows, block), lambda: (0, 0))] * size,
        out_shape=[part] * size,
        compiler_params=pltpu.CompilerParams(vmem_limit_bytes=VMEM_BYTES),
        cost_estimate=pl.CostEstimate(
            flops=2 * rows * width * block * size,
            bytes_accessed=2 * width * block * size,
            transcendentals=0,
        ),
        name="project",
    )(chunk, *terms, key_proj, value_proj)


def pieces_of(blocks, cuts):
    height = sum(cuts)
    starts = [sum(cuts[:c]) for c in range(len(cuts))]
    whole = blocks[0].shape[0] // height
    rows = [
        block[i * height + start : i * height + start + cut]
        for start, cut in zip(starts, cuts)
        for block in blocks
        for i in range(whole)
    ]
    count = len(blocks) * whole
    return jnp.concatenate(rows, 0), [(count * start, count * cut) for start, cut in zip(starts, cuts)]


def back_kernel(count, cuts, chunk_ref, *refs):
    states, downs, out_refs = refs[:count], refs[count : count + 2], refs[count + 2 :]
    size, _, hidden = out_refs[0].shape
    hidden = hidden // 2
    state, places = pieces_of([ref[...] for ref in states], cuts)
    for k in range(size):
        at = pl.ds(pl.multiple_of(chunk_ref[k] * hidden, hidden), hidden)
        for i in range(2):
            part = dot(state, downs[i][at, :], NT).astype(BF16)
            for (start, rows), out_ref in zip(places, out_refs):
                out_ref[k, :, i * hidden : (i + 1) * hidden] = part[start : start + rows]


def back_parts(chunk, states, downs, cuts):
    size, (height, width) = chunk.shape[0], states[0].shape
    count = len(states)
    if height % 16:
        states = [jnp.concatenate(states, 0)]
    hidden = downs[0].shape[0] // size
    return pl.pallas_call(
        functools.partial(back_kernel, len(states), cuts),
        in_specs=[pl.BlockSpec(memory_space=pltpu.SMEM)]
        + [pl.BlockSpec(memory_space=pltpu.VMEM)] * (len(states) + 2),
        out_shape=[jax.ShapeDtypeStruct((size, count * cut, 2 * hidden), BF16) for cut in cuts],
        compiler_params=pltpu.CompilerParams(vmem_limit_bytes=VMEM_BYTES),
        cost_estimate=pl.CostEstimate(
            flops=4 * count * height * width * hidden * size,
            bytes_accessed=4 * width * hidden * size,
            transcendentals=0,
        ),
        name="back",
    )(chunk, *states, *downs)


def pre_kernel(count, cuts, *refs):
    inputs, ups, out_refs = refs[:count], refs[count : count + 2], refs[len(refs) - len(cuts) :]
    hidden = out_refs[0].shape[1] // 2
    size = ups[0].shape[0]
    whole = [pieces_of([ref[k] for ref in inputs], cuts) for k in range(size)]
    for i in range(2):
        part = sum(dot(whole[k][0], ups[i][k, :hidden, :], NT) for k in range(size))
        for (start, rows), out_ref in zip(whole[0][1], out_refs):
            out_ref[:, i * hidden : (i + 1) * hidden] = part[start : start + rows]


def pre_parts(inputs, ups, hidden, cuts, after):
    count, height = len(inputs), inputs[0].shape[1]
    if height % 16:
        inputs = [jnp.concatenate(inputs, 1)]
    return pl.pallas_call(
        functools.partial(pre_kernel, len(inputs), cuts),
        in_specs=[pl.BlockSpec(x.shape, lambda: (0, 0, 0)) for x in (*inputs, *ups)]
        + [pl.BlockSpec(memory_space=pl.ANY)] * len(after),
        out_shape=[jax.ShapeDtypeStruct((count * cut, 2 * hidden), F32) for cut in cuts],
        compiler_params=pltpu.CompilerParams(vmem_limit_bytes=VMEM_BYTES),
        cost_estimate=pl.CostEstimate(
            flops=4 * count * height * hidden * ups[0].shape[0] * ups[0].shape[2],
            bytes_accessed=4 * ups[0].size,
            transcendentals=0,
        ),
        name="pre",
    )(*inputs, *ups, *after)


def feed_kernel(count, chunk_ref, *refs):
    terms, slope_ref, ups, out_ref = refs[:count], refs[count], refs[count + 1 : count + 3], refs[-1]
    back = sum(ref[...].astype(F32) for ref in terms)
    gated = (slope_ref[...] * back).astype(BF16)
    hidden = gated.shape[1] // 2
    size, _, width = ups[0].shape
    for k in range(size):
        part = sum(
            dot(gated[:, i * hidden : (i + 1) * hidden], ups[i][chunk_ref[k], :hidden, :], NN)
            for i in range(2)
        )
        out_ref[:, :, k * width : (k + 1) * width] = part.astype(BF16).reshape(
            out_ref.shape[0], out_ref.shape[1], width
        )


def feed(chunk, terms, slope, ups, blocks):
    rows = terms[0].shape[0]
    size, _, width = ups[0].shape
    hidden = terms[0].shape[1] // 2
    return pl.pallas_call(
        functools.partial(feed_kernel, len(terms)),
        in_specs=[pl.BlockSpec(memory_space=pltpu.SMEM)]
        + [pl.BlockSpec(memory_space=pltpu.VMEM)] * (len(terms) + 3),
        out_specs=pl.BlockSpec(memory_space=pltpu.VMEM),
        out_shape=jax.ShapeDtypeStruct((blocks, rows // blocks, size * width), BF16),
        compiler_params=pltpu.CompilerParams(vmem_limit_bytes=VMEM_BYTES),
        cost_estimate=pl.CostEstimate(
            flops=4 * rows * hidden * width * size,
            bytes_accessed=4 * hidden * width * size,
            transcendentals=0,
        ),
        name="feed",
    )(chunk, *terms, slope, *ups)


def local(queries, keys, values, out_grad, key_proj, value_proj, global_in, up_proj, down_proj):
    size, planes = lax.axis_size("seq"), lax.axis_size("heads")
    place = lax.axis_index("seq") ^ jnp.arange(size, dtype=jnp.int32)
    chunk = lax.axis_index("heads") ^ jnp.arange(planes, dtype=jnp.int32)
    far = size // 2
    rows, width = global_in.shape
    cuts = (rows // 2, rows // 2) if rows % 32 == 0 else (rows,)

    downs = [down_proj, swap(down_proj, "seq", 1)]
    hidden = up_proj.shape[1] // planes
    own_up = lax.all_to_all(bundle(up_proj, global_in, planes), "heads", 0, 0)

    arrays = (queries, out_grad, keys, values)
    heads = queries.shape[1] // HD
    query_grad, even, odd = attend(place, *arrays, 0, heads)
    terms = scatter_rows([even], [odd], [])
    terms[0], downs[1] = lax.optimization_barrier((terms[0], downs[1]))
    near = prepare([value_proj], terms[:1])
    share = list(project(chunk, terms, key_proj, *near))
    own_up, share[0] = lax.optimization_barrier((own_up, share[0]))
    ups = [own_up, swap(own_up, "seq", 1)]
    shares = [share[0]] + [swap(share[k], "heads", k) for k in range(1, planes)]
    shares, ups[1] = lax.optimization_barrier((shares, ups[1]))
    state = sum(t.astype(F32) for t in shares)
    state_low = state.astype(BF16)
    inputs = gather_blocks(own_up[:, hidden:], "seq", 2, far)
    states = gather_blocks(state_low, "seq", 2, far)
    parts = back_parts(chunk, states, downs, cuts)
    slopes = [slope_of(pre) for pre in pre_parts(inputs, ups, hidden, cuts, parts[:1])]

    grads = []
    for part, slope in zip(parts, slopes):
        terms = [part[0]] + [swap(part[k], "heads", k) for k in range(1, planes)]
        grown = feed(chunk, terms, slope, ups, far)
        own = sum(t.astype(F32) for t in scatter_terms([grown[j] for j in range(far)], "seq", 2))
        blocks = [own[:, k * width : (k + 1) * width] for k in range(planes)]
        grads.append(
            blocks[0]
            + sum(swap(blocks[k].astype(BF16), "heads", k).astype(F32) for k in range(1, planes))
        )
    global_grad = state + jnp.concatenate(grads, 0)
    return (query_grad, global_grad)


def solution(mesh):
    placed = (
        P("seq", "heads"),
        P(None, "heads"),
        P(None, "heads"),
        P("seq", "heads"),
        P(None, "heads"),
        P(None, "heads"),
        P("seq", "heads"),
        P("heads", "seq"),
        P("seq", "heads"),
    )
    return jax.shard_map(
        local,
        mesh=mesh,
        in_specs=placed,
        out_specs=(P("seq", "heads"), P("seq", "heads")),
        check_vma=False,
    )
```

```python
import functools
import math

import jax
import jax.numpy as jnp
from jax import lax
from jax.experimental import pallas as pl
from jax.experimental.pallas import tpu as pltpu
from jax.sharding import PartitionSpec as P

HD = 128
SCALE = HD**-0.5
SCALE_LOG2 = SCALE * math.log2(math.e)
BF16, F32 = jnp.bfloat16, jnp.float32
NT = (((1,), (1,)), ((), ()))
NN = (((1,), (0,)), ((), ()))
TN = (((0,), (0,)), ((), ()))
VMEM_BYTES = 24 * 2**20


def dot(a, b, dims):
    return lax.dot_general(a, b, dims, preferred_element_type=F32)


def slope_of(pre):
    return (
        0.5 * (1.0 + lax.erf(pre * 0.7071067811865476))
        + pre * jnp.exp(-0.5 * pre * pre) * 0.3989422804014327
    )


def swap(x, axis, distance):
    size = lax.axis_size(axis)
    return lax.ppermute(x, axis, [(i, i ^ distance) for i in range(size)])


def levels_of(first, count):
    levels = []
    while count > 1:
        radix = min(4, count)
        levels.append((first, radix))
        first, count = first * radix, count // radix
    return levels


def gather_blocks(x, axis, first, count):
    blocks = [x]
    for step, radix in levels_of(first, count):
        whole = blocks[0] if len(blocks) == 1 else jnp.stack(blocks)
        got = [swap(whole, axis, step * k) for k in range(1, radix)]
        for other in got:
            blocks = blocks + ([other] if whole is x else list(other))
    return blocks


def scatter_terms(blocks, axis, first, low=BF16):
    levels = levels_of(first, len(blocks))
    for step, radix in reversed(levels[1:]):
        span = step // first
        terms = [blocks[k * span : (k + 1) * span] for k in range(radix)]
        got = [swap(jnp.stack(terms[k]), axis, step * k) for k in range(1, radix)]
        blocks = [
            (terms[0][i].astype(F32) + sum(g[i].astype(F32) for g in got)).astype(low)
            for i in range(span)
        ]
    return [blocks[0]] + [swap(blocks[k], axis, first * k) for k in range(1, len(blocks))]


def attend_kernel(sub, place_ref, q_ref, g_ref, k_ref, v_ref, *rest):
    dq_ref, even_ref, odd_ref, acc_ref = rest[-4:]
    block = pl.program_id(1)
    keys, values = k_ref[...], v_ref[...]

    @pl.when(block == 0)
    def _():
        acc_ref[...] = jnp.zeros_like(acc_ref)

    def products(at):
        return dot(keys, q_ref[at, :], NT), dot(values, g_ref[at, :], NT)

    def soften(scores, weight_grad):
        top = jnp.max(scores, axis=0, keepdims=True)
        grown = jnp.exp2((scores - top) * SCALE_LOG2)
        weights = grown * (1.0 / jnp.sum(grown, axis=0, keepdims=True))
        centre = jnp.sum(weights * weight_grad, axis=0, keepdims=True)
        return (weights * (weight_grad - centre)).astype(BF16), weights.astype(BF16)

    def collect(at, score_grad, weights_low):
        dq_ref[at, :] = (SCALE * dot(keys, score_grad, TN)).T.astype(BF16)
        acc_ref[:, :HD] += dot(score_grad, q_ref[at, :], NN)
        acc_ref[:, HD:] += dot(weights_low, g_ref[at, :], NN)

    pieces = [pl.ds(i * sub, sub) for i in range(q_ref.shape[0] // sub)]
    ahead, behind = products(pieces[0]), None
    for i, at in enumerate(pieces):
        now, ahead = ahead, products(pieces[i + 1]) if i + 1 < len(pieces) else None
        if behind is not None:
            collect(pieces[i - 1], *behind)
        behind = soften(*now)
    collect(pieces[-1], *behind)

    @pl.when(block == pl.num_programs(1) - 1)
    def _():
        acc_ref[:, :HD] = SCALE * acc_ref[:, :HD]
        half, height = even_ref.shape[:2]
        for j in range(2 * half):
            at = pl.ds(pl.multiple_of(place_ref[j] * height, height), height)
            (odd_ref if j % 2 else even_ref)[j // 2] = acc_ref[at, :].astype(BF16)


def attend(place, queries, out_grad, keys, values, first, count, query_grad=None, after=()):
    tokens, width = queries.shape
    glob, size = keys.shape[0], place.shape[0]
    block = min(2048, tokens)
    token_spec = pl.BlockSpec((block, HD), lambda h, b, place: (b, h + first))
    global_spec = pl.BlockSpec((glob, HD), lambda h, b, place: (0, h + first))
    part_spec = pl.BlockSpec((size // 2, glob // size, 2 * HD), lambda h, b, place: (0, 0, h))
    part = pltpu.VMEM((size // 2, glob // size, 2 * HD * count), BF16)
    extra = [x for x in (query_grad, *after) if x is not None]
    return pl.pallas_call(
        functools.partial(attend_kernel, min(256, block)),
        grid_spec=pltpu.PrefetchScalarGridSpec(
            num_scalar_prefetch=1,
            grid=(count, tokens // block),
            in_specs=[token_spec, token_spec, global_spec, global_spec]
            + [pl.BlockSpec(memory_space=pl.ANY)] * len(extra),
            out_specs=[token_spec, part_spec, part_spec],
            scratch_shapes=[pltpu.VMEM((glob, 2 * HD), F32)],
        ),
        out_shape=[pltpu.HBM((tokens, width), BF16), part, part],
        input_output_aliases={} if query_grad is None else {5: 0},
        compiler_params=pltpu.CompilerParams(vmem_limit_bytes=VMEM_BYTES),
        cost_estimate=pl.CostEstimate(
            flops=20 * tokens * glob * HD * count,
            bytes_accessed=6 * tokens * HD * count,
            transcendentals=tokens * glob * count,
        ),
        name="attend",
    )(place, *map(hold, (queries, out_grad, keys, values)), *extra)


def hold(x):
    return pltpu.with_memory_space_constraint(x, pltpu.HBM)


def bundle_kernel(up_ref, in_ref, out_ref):
    size, depth, _ = out_ref.shape
    rows = in_ref.shape[0]
    hidden = depth - rows
    for k in range(size):
        out_ref[k, :hidden, :] = up_ref[:, k * hidden : (k + 1) * hidden].T
        out_ref[k, hidden:, :] = in_ref[...]


def bundle(up_proj, global_in, size):
    (width, hidden), rows = up_proj.shape, global_in.shape[0]
    if (hidden // size) % 128 or rows % 16:
        return jnp.concatenate(
            [
                up_proj.T.reshape(size, hidden // size, width),
                jnp.broadcast_to(global_in[None], (size, rows, width)),
            ],
            1,
        )
    return pl.pallas_call(
        bundle_kernel,
        out_shape=jax.ShapeDtypeStruct((size, hidden // size + rows, width), BF16),
        compiler_params=pltpu.CompilerParams(vmem_limit_bytes=VMEM_BYTES),
        cost_estimate=pl.CostEstimate(
            flops=0, bytes_accessed=4 * up_proj.size, transcendentals=0
        ),
        name="bundle",
    )(hold(up_proj), hold(global_in))


def merge_kernel(count, *refs):
    evens, gots = refs[:count], refs[count : 2 * count]
    out_refs = refs[len(refs) - evens[0].shape[0] :]
    at = 0
    for even_ref, got_ref in zip(evens, gots):
        cols = pl.ds(at, even_ref.shape[2])
        at += even_ref.shape[2]
        for j, out_ref in enumerate(out_refs):
            out_ref[:, cols] = (even_ref[j].astype(F32) + got_ref[j].astype(F32)).astype(BF16)


def scatter_rows(evens, odds, near):
    gots = [swap(odd, "seq", 1) for odd in odds]
    blocks, rows, _ = evens[0].shape
    width = sum(even.shape[2] for even in evens)
    spec = lambda x: pl.BlockSpec(x.shape, lambda: (0, 0, 0))
    mine = pl.pallas_call(
        functools.partial(merge_kernel, len(evens)),
        in_specs=[spec(x) for x in (*evens, *gots)]
        + [pl.BlockSpec(memory_space=pltpu.VMEM)] * len(near),
        out_shape=[pltpu.VMEM((rows, width), BF16)] * blocks,
        compiler_params=pltpu.CompilerParams(vmem_limit_bytes=VMEM_BYTES),
        cost_estimate=pl.CostEstimate(
            flops=blocks * rows * width, bytes_accessed=6 * blocks * rows * width, transcendentals=0
        ),
        name="merge",
    )(*evens, *gots, *near)
    return scatter_terms(mine, "seq", 2)


def prepare_kernel(*refs):
    half = len(refs) // 2
    for from_ref, to_ref in zip(refs[:half], refs[half:]):
        to_ref[...] = from_ref[...].T


def prepare(arrays, after):
    count = len(arrays)
    return pl.pallas_call(
        lambda *refs: prepare_kernel(*refs[:count], *refs[count + len(after) :]),
        grid=(4,),
        in_specs=[pl.BlockSpec((x.shape[0] // 4, x.shape[1]), lambda i: (i, 0)) for x in arrays]
        + [pl.BlockSpec(memory_space=pl.ANY)] * len(after),
        out_specs=[pl.BlockSpec((x.shape[1], x.shape[0] // 4), lambda i: (0, i)) for x in arrays],
        out_shape=[pltpu.VMEM(x.shape[::-1], x.dtype) for x in arrays],
        compiler_params=pltpu.CompilerParams(vmem_limit_bytes=VMEM_BYTES),
        cost_estimate=pl.CostEstimate(
            flops=0, bytes_accessed=4 * arrays[0].size, transcendentals=0
        ),
        name="prepare",
    )(*map(hold, arrays), *after)


def project_kernel(count, chunk_ref, *refs):
    terms, (key_proj_ref, value_proj_ref) = refs[:count], refs[count : count + 2]
    part_refs = refs[count + 2 :]
    total = sum(t[...].astype(F32) for t in terms).astype(BF16)
    heads = total.shape[1] // (2 * HD)
    pick = lambda at: [total[:, (2 * h + at) * HD : (2 * h + at + 1) * HD] for h in range(heads)]
    key_low, value_low = jnp.concatenate(pick(0), 1), jnp.concatenate(pick(1), 1)
    block = part_refs[0].shape[1]
    for k, part_ref in enumerate(part_refs):
        at = pl.ds(pl.multiple_of(chunk_ref[k] * block, block), block)
        part = dot(key_low, key_proj_ref[at, :], NT) + dot(value_low, value_proj_ref[:, at], NN)
        part_ref[...] = part.astype(BF16)


def project(chunk, terms, key_proj, value_proj):
    rows, width = terms[0].shape
    size = chunk.shape[0]
    block = key_proj.shape[0] // size
    part = pltpu.HBM((rows, block), BF16)
    return pl.pallas_call(
        functools.partial(project_kernel, len(terms)),
        in_specs=[pl.BlockSpec(memory_space=pltpu.SMEM)]
        + [pl.BlockSpec(memory_space=pltpu.VMEM)] * (len(terms) + 2),
        out_specs=[pl.BlockSpec((rows, block), lambda: (0, 0))] * size,
        out_shape=[part] * size,
        compiler_params=pltpu.CompilerParams(vmem_limit_bytes=VMEM_BYTES),
        cost_estimate=pl.CostEstimate(
            flops=2 * rows * width * block * size,
            bytes_accessed=2 * width * block * size,
            transcendentals=0,
        ),
        name="project",
    )(chunk, *terms, key_proj, value_proj)


def pieces_of(blocks, cuts):
    height = sum(cuts)
    starts = [sum(cuts[:c]) for c in range(len(cuts))]
    whole = blocks[0].shape[0] // height
    rows = [
        block[i * height + start : i * height + start + cut]
        for start, cut in zip(starts, cuts)
        for block in blocks
        for i in range(whole)
    ]
    count = len(blocks) * whole
    return jnp.concatenate(rows, 0), [(count * start, count * cut) for start, cut in zip(starts, cuts)]


def back_kernel(count, cuts, chunk_ref, *refs):
    states, downs, out_refs = refs[:count], refs[count : count + 2], refs[count + 2 :]
    size, _, hidden = out_refs[0].shape
    hidden = hidden // 2
    state, places = pieces_of([ref[...] for ref in states], cuts)
    for k in range(size):
        at = pl.ds(pl.multiple_of(chunk_ref[k] * hidden, hidden), hidden)
        for i in range(2):
            part = dot(state, downs[i][at, :], NT).astype(BF16)
            for (start, rows), out_ref in zip(places, out_refs):
                out_ref[k, :, i * hidden : (i + 1) * hidden] = part[start : start + rows]


def back_parts(chunk, states, downs, cuts):
    size, (height, width) = chunk.shape[0], states[0].shape
    count = len(states)
    if height % 16:
        states = [jnp.concatenate(states, 0)]
    hidden = downs[0].shape[0] // size
    return pl.pallas_call(
        functools.partial(back_kernel, len(states), cuts),
        in_specs=[pl.BlockSpec(memory_space=pltpu.SMEM)]
        + [pl.BlockSpec(memory_space=pltpu.VMEM)] * (len(states) + 2),
        out_shape=[jax.ShapeDtypeStruct((size, count * cut, 2 * hidden), BF16) for cut in cuts],
        compiler_params=pltpu.CompilerParams(vmem_limit_bytes=VMEM_BYTES),
        cost_estimate=pl.CostEstimate(
            flops=4 * count * height * width * hidden * size,
            bytes_accessed=4 * width * hidden * size,
            transcendentals=0,
        ),
        name="back",
    )(chunk, *states, *downs)


def pre_kernel(count, cuts, *refs):
    inputs, ups, out_refs = refs[:count], refs[count : count + 2], refs[len(refs) - len(cuts) :]
    hidden = out_refs[0].shape[1] // 2
    size = ups[0].shape[0]
    whole = [pieces_of([ref[k] for ref in inputs], cuts) for k in range(size)]
    for i in range(2):
        part = sum(dot(whole[k][0], ups[i][k, :hidden, :], NT) for k in range(size))
        for (start, rows), out_ref in zip(whole[0][1], out_refs):
            out_ref[:, i * hidden : (i + 1) * hidden] = part[start : start + rows]


def pre_parts(inputs, ups, hidden, cuts, after):
    count, height = len(inputs), inputs[0].shape[1]
    if height % 16:
        inputs = [jnp.concatenate(inputs, 1)]
    return pl.pallas_call(
        functools.partial(pre_kernel, len(inputs), cuts),
        in_specs=[pl.BlockSpec(x.shape, lambda: (0, 0, 0)) for x in (*inputs, *ups)]
        + [pl.BlockSpec(memory_space=pl.ANY)] * len(after),
        out_shape=[jax.ShapeDtypeStruct((count * cut, 2 * hidden), F32) for cut in cuts],
        compiler_params=pltpu.CompilerParams(vmem_limit_bytes=VMEM_BYTES),
        cost_estimate=pl.CostEstimate(
            flops=4 * count * height * hidden * ups[0].shape[0] * ups[0].shape[2],
            bytes_accessed=4 * ups[0].size,
            transcendentals=0,
        ),
        name="pre",
    )(*inputs, *ups, *after)


def feed_kernel(count, chunk_ref, *refs):
    terms, slope_ref, ups, out_ref = refs[:count], refs[count], refs[count + 1 : count + 3], refs[-1]
    back = sum(ref[...].astype(F32) for ref in terms)
    gated = (slope_ref[...] * back).astype(BF16)
    hidden = gated.shape[1] // 2
    size, _, width = ups[0].shape
    for k in range(size):
        part = sum(
            dot(gated[:, i * hidden : (i + 1) * hidden], ups[i][chunk_ref[k], :hidden, :], NN)
            for i in range(2)
        )
        out_ref[:, :, k * width : (k + 1) * width] = part.astype(BF16).reshape(
            out_ref.shape[0], out_ref.shape[1], width
        )


def feed(chunk, terms, slope, ups, blocks):
    rows = terms[0].shape[0]
    size, _, width = ups[0].shape
    hidden = terms[0].shape[1] // 2
    return pl.pallas_call(
        functools.partial(feed_kernel, len(terms)),
        in_specs=[pl.BlockSpec(memory_space=pltpu.SMEM)]
        + [pl.BlockSpec(memory_space=pltpu.VMEM)] * (len(terms) + 3),
        out_specs=pl.BlockSpec(memory_space=pltpu.VMEM),
        out_shape=jax.ShapeDtypeStruct((blocks, rows // blocks, size * width), BF16),
        compiler_params=pltpu.CompilerParams(vmem_limit_bytes=VMEM_BYTES),
        cost_estimate=pl.CostEstimate(
            flops=4 * rows * hidden * width * size,
            bytes_accessed=4 * hidden * width * size,
            transcendentals=0,
        ),
        name="feed",
    )(chunk, *terms, slope, *ups)


def local(queries, keys, values, out_grad, key_proj, value_proj, global_in, up_proj, down_proj):
    size, planes = lax.axis_size("seq"), lax.axis_size("heads")
    place = lax.axis_index("seq") ^ jnp.arange(size, dtype=jnp.int32)
    chunk = lax.axis_index("heads") ^ jnp.arange(planes, dtype=jnp.int32)
    far = size // 2
    rows, width = global_in.shape
    cuts = (rows // 2, rows // 2) if rows % 32 == 0 else (rows,)

    downs = [down_proj, swap(down_proj, "seq", 1)]
    hidden = up_proj.shape[1] // planes
    own_up = lax.all_to_all(bundle(up_proj, global_in, planes), "heads", 0, 0)

    arrays = (queries, out_grad, keys, values)
    heads = queries.shape[1] // HD
    query_grad, even, odd = attend(place, *arrays, 0, heads)
    terms = scatter_rows([even], [odd], [])
    terms[0], downs[1] = lax.optimization_barrier((terms[0], downs[1]))
    near = prepare([value_proj], terms[:1])
    share = list(project(chunk, terms, key_proj, *near))
    own_up, share[0] = lax.optimization_barrier((own_up, share[0]))
    ups = [own_up, swap(own_up, "seq", 1)]
    shares = [share[0]] + [swap(share[k], "heads", k) for k in range(1, planes)]
    shares, ups[1] = lax.optimization_barrier((shares, ups[1]))
    state = sum(t.astype(F32) for t in shares)
    state_low = state.astype(BF16)
    inputs = gather_blocks(own_up[:, hidden:], "seq", 2, far)
    states = gather_blocks(state_low, "seq", 2, far)
    parts = back_parts(chunk, states, downs, cuts)
    slopes = [slope_of(pre) for pre in pre_parts(inputs, ups, hidden, cuts, parts[:1])]

    grads = []
    for part, slope in zip(parts, slopes):
        terms = [part[0]] + [swap(part[k], "heads", k) for k in range(1, planes)]
        grown = feed(chunk, terms, slope, ups, far)
        own = sum(t.astype(F32) for t in scatter_terms([grown[j] for j in range(far)], "seq", 2))
        blocks = [own[:, k * width : (k + 1) * width] for k in range(planes)]
        grads.append(
            blocks[0]
            + sum(swap(blocks[k].astype(BF16), "heads", k).astype(F32) for k in range(1, planes))
        )
    global_grad = state + jnp.concatenate(grads, 0)
    return (query_grad, global_grad)


def solution(mesh):
    placed = (
        P("seq", "heads"),
        P(None, "heads"),
        P(None, "heads"),
        P("seq", "heads"),
        P(None, "heads"),
        P(None, "heads"),
        P("seq", "heads"),
        P("heads", "seq"),
        P("seq", "heads"),
    )
    return jax.shard_map(
        local,
        mesh=mesh,
        in_specs=placed,
        out_specs=(P("seq", "heads"), P("seq", "heads")),
        check_vma=False,
    )
```

```python
import functools
import math

import jax
import jax.numpy as jnp
from jax import lax
from jax.experimental import pallas as pl
from jax.experimental.pallas import tpu as pltpu
from jax.sharding import PartitionSpec as P

HD = 128
SCALE = HD**-0.5
SCALE_LOG2 = SCALE * math.log2(math.e)
BF16, F32 = jnp.bfloat16, jnp.float32
NT = (((1,), (1,)), ((), ()))
NN = (((1,), (0,)), ((), ()))
TN = (((0,), (0,)), ((), ()))
VMEM_BYTES = 24 * 2**20


def dot(a, b, dims):
    return lax.dot_general(a, b, dims, preferred_element_type=F32)


def slope_of(pre):
    return (
        0.5 * (1.0 + lax.erf(pre * 0.7071067811865476))
        + pre * jnp.exp(-0.5 * pre * pre) * 0.3989422804014327
    )


def swap(x, axis, distance):
    size = lax.axis_size(axis)
    return lax.ppermute(x, axis, [(i, i ^ distance) for i in range(size)])


def levels_of(first, count):
    levels = []
    while count > 1:
        radix = min(4, count)
        levels.append((first, radix))
        first, count = first * radix, count // radix
    return levels


def gather_blocks(x, axis, first, count):
    blocks = [x]
    for step, radix in levels_of(first, count):
        whole = blocks[0] if len(blocks) == 1 else jnp.stack(blocks)
        got = [swap(whole, axis, step * k) for k in range(1, radix)]
        for other in got:
            blocks = blocks + ([other] if whole is x else list(other))
    return blocks


def scatter_terms(blocks, axis, first, low=BF16):
    levels = levels_of(first, len(blocks))
    for step, radix in reversed(levels[1:]):
        span = step // first
        terms = [blocks[k * span : (k + 1) * span] for k in range(radix)]
        got = [swap(jnp.stack(terms[k]), axis, step * k) for k in range(1, radix)]
        blocks = [
            (terms[0][i].astype(F32) + sum(g[i].astype(F32) for g in got)).astype(low)
            for i in range(span)
        ]
    return [blocks[0]] + [swap(blocks[k], axis, first * k) for k in range(1, len(blocks))]


def attend_kernel(sub, place_ref, q_ref, g_ref, k_ref, v_ref, *rest):
    dq_ref, even_ref, odd_ref, acc_ref = rest[-4:]
    block = pl.program_id(1)
    keys, values = k_ref[...], v_ref[...]

    @pl.when(block == 0)
    def _():
        acc_ref[...] = jnp.zeros_like(acc_ref)

    def products(at):
        return dot(keys, q_ref[at, :], NT), dot(values, g_ref[at, :], NT)

    def soften(scores, weight_grad):
        top = jnp.max(scores, axis=0, keepdims=True)
        grown = jnp.exp2((scores - top) * SCALE_LOG2)
        weights = grown * (1.0 / jnp.sum(grown, axis=0, keepdims=True))
        centre = jnp.sum(weights * weight_grad, axis=0, keepdims=True)
        return (weights * (weight_grad - centre)).astype(BF16), weights.astype(BF16)

    def collect(at, score_grad, weights_low):
        dq_ref[at, :] = (SCALE * dot(keys, score_grad, TN)).T.astype(BF16)
        acc_ref[:, :HD] += dot(score_grad, q_ref[at, :], NN)
        acc_ref[:, HD:] += dot(weights_low, g_ref[at, :], NN)

    pieces = [pl.ds(i * sub, sub) for i in range(q_ref.shape[0] // sub)]
    ahead, behind = products(pieces[0]), None
    for i, at in enumerate(pieces):
        now, ahead = ahead, products(pieces[i + 1]) if i + 1 < len(pieces) else None
        if behind is not None:
            collect(pieces[i - 1], *behind)
        behind = soften(*now)
    collect(pieces[-1], *behind)

    @pl.when(block == pl.num_programs(1) - 1)
    def _():
        acc_ref[:, :HD] = SCALE * acc_ref[:, :HD]
        half, height = even_ref.shape[:2]
        for j in range(2 * half):
            at = pl.ds(pl.multiple_of(place_ref[j] * height, height), height)
            (odd_ref if j % 2 else even_ref)[j // 2] = acc_ref[at, :].astype(BF16)


def attend(place, queries, out_grad, keys, values, first, count, query_grad=None, after=()):
    tokens, width = queries.shape
    glob, size = keys.shape[0], place.shape[0]
    block = min(2048, tokens)
    token_spec = pl.BlockSpec((block, HD), lambda h, b, place: (b, h + first))
    global_spec = pl.BlockSpec((glob, HD), lambda h, b, place: (0, h + first))
    part_spec = pl.BlockSpec((size // 2, glob // size, 2 * HD), lambda h, b, place: (0, 0, h))
    part = pltpu.VMEM((size // 2, glob // size, 2 * HD * count), BF16)
    extra = [x for x in (query_grad, *after) if x is not None]
    return pl.pallas_call(
        functools.partial(attend_kernel, min(256, block)),
        grid_spec=pltpu.PrefetchScalarGridSpec(
            num_scalar_prefetch=1,
            grid=(count, tokens // block),
            in_specs=[token_spec, token_spec, global_spec, global_spec]
            + [pl.BlockSpec(memory_space=pl.ANY)] * len(extra),
            out_specs=[token_spec, part_spec, part_spec],
            scratch_shapes=[pltpu.VMEM((glob, 2 * HD), F32)],
        ),
        out_shape=[pltpu.HBM((tokens, width), BF16), part, part],
        input_output_aliases={} if query_grad is None else {5: 0},
        compiler_params=pltpu.CompilerParams(vmem_limit_bytes=VMEM_BYTES),
        cost_estimate=pl.CostEstimate(
            flops=20 * tokens * glob * HD * count,
            bytes_accessed=6 * tokens * HD * count,
            transcendentals=tokens * glob * count,
        ),
        name="attend",
    )(place, *map(hold, (queries, out_grad, keys, values)), *extra)


def hold(x):
    return pltpu.with_memory_space_constraint(x, pltpu.HBM)


def bundle_kernel(up_ref, in_ref, out_ref):
    size, depth, _ = out_ref.shape
    rows = in_ref.shape[0]
    hidden = depth - rows
    for k in range(size):
        out_ref[k, :hidden, :] = up_ref[:, k * hidden : (k + 1) * hidden].T
        out_ref[k, hidden:, :] = in_ref[...]


def bundle(up_proj, global_in, size):
    (width, hidden), rows = up_proj.shape, global_in.shape[0]
    if (hidden // size) % 128 or rows % 16:
        return jnp.concatenate(
            [
                up_proj.T.reshape(size, hidden // size, width),
                jnp.broadcast_to(global_in[None], (size, rows, width)),
            ],
            1,
        )
    return pl.pallas_call(
        bundle_kernel,
        out_shape=jax.ShapeDtypeStruct((size, hidden // size + rows, width), BF16),
        compiler_params=pltpu.CompilerParams(vmem_limit_bytes=VMEM_BYTES),
        cost_estimate=pl.CostEstimate(
            flops=0, bytes_accessed=4 * up_proj.size, transcendentals=0
        ),
        name="bundle",
    )(hold(up_proj), hold(global_in))


def merge_kernel(count, *refs):
    evens, gots = refs[:count], refs[count : 2 * count]
    out_refs = refs[len(refs) - evens[0].shape[0] :]
    at = 0
    for even_ref, got_ref in zip(evens, gots):
        cols = pl.ds(at, even_ref.shape[2])
        at += even_ref.shape[2]
        for j, out_ref in enumerate(out_refs):
            out_ref[:, cols] = (even_ref[j].astype(F32) + got_ref[j].astype(F32)).astype(BF16)


def scatter_rows(evens, odds, near):
    gots = [swap(odd, "seq", 1) for odd in odds]
    blocks, rows, _ = evens[0].shape
    width = sum(even.shape[2] for even in evens)
    spec = lambda x: pl.BlockSpec(x.shape, lambda: (0, 0, 0))
    mine = pl.pallas_call(
        functools.partial(merge_kernel, len(evens)),
        in_specs=[spec(x) for x in (*evens, *gots)]
        + [pl.BlockSpec(memory_space=pltpu.VMEM)] * len(near),
        out_shape=[pltpu.VMEM((rows, width), BF16)] * blocks,
        compiler_params=pltpu.CompilerParams(vmem_limit_bytes=VMEM_BYTES),
        cost_estimate=pl.CostEstimate(
            flops=blocks * rows * width, bytes_accessed=6 * blocks * rows * width, transcendentals=0
        ),
        name="merge",
    )(*evens, *gots, *near)
    return scatter_terms(mine, "seq", 2)


def prepare_kernel(*refs):
    half = len(refs) // 2
    for from_ref, to_ref in zip(refs[:half], refs[half:]):
        to_ref[...] = from_ref[...].T


def prepare(arrays, after):
    count = len(arrays)
    return pl.pallas_call(
        lambda *refs: prepare_kernel(*refs[:count], *refs[count + len(after) :]),
        grid=(4,),
        in_specs=[pl.BlockSpec((x.shape[0] // 4, x.shape[1]), lambda i: (i, 0)) for x in arrays]
        + [pl.BlockSpec(memory_space=pl.ANY)] * len(after),
        out_specs=[pl.BlockSpec((x.shape[1], x.shape[0] // 4), lambda i: (0, i)) for x in arrays],
        out_shape=[pltpu.VMEM(x.shape[::-1], x.dtype) for x in arrays],
        compiler_params=pltpu.CompilerParams(vmem_limit_bytes=VMEM_BYTES),
        cost_estimate=pl.CostEstimate(
            flops=0, bytes_accessed=4 * arrays[0].size, transcendentals=0
        ),
        name="prepare",
    )(*map(hold, arrays), *after)


def project_kernel(count, chunk_ref, *refs):
    terms, (key_proj_ref, value_proj_ref) = refs[:count], refs[count : count + 2]
    part_refs = refs[count + 2 :]
    total = sum(t[...].astype(F32) for t in terms).astype(BF16)
    heads = total.shape[1] // (2 * HD)
    pick = lambda at: [total[:, (2 * h + at) * HD : (2 * h + at + 1) * HD] for h in range(heads)]
    key_low, value_low = jnp.concatenate(pick(0), 1), jnp.concatenate(pick(1), 1)
    block = part_refs[0].shape[1]
    for k, part_ref in enumerate(part_refs):
        at = pl.ds(pl.multiple_of(chunk_ref[k] * block, block), block)
        part = dot(key_low, key_proj_ref[at, :], NT) + dot(value_low, value_proj_ref[:, at], NN)
        part_ref[...] = part.astype(BF16)


def project(chunk, terms, key_proj, value_proj):
    rows, width = terms[0].shape
    size = chunk.shape[0]
    block = key_proj.shape[0] // size
    part = pltpu.HBM((rows, block), BF16)
    return pl.pallas_call(
        functools.partial(project_kernel, len(terms)),
        in_specs=[pl.BlockSpec(memory_space=pltpu.SMEM)]
        + [pl.BlockSpec(memory_space=pltpu.VMEM)] * (len(terms) + 2),
        out_specs=[pl.BlockSpec((rows, block), lambda: (0, 0))] * size,
        out_shape=[part] * size,
        compiler_params=pltpu.CompilerParams(vmem_limit_bytes=VMEM_BYTES),
        cost_estimate=pl.CostEstimate(
            flops=2 * rows * width * block * size,
            bytes_accessed=2 * width * block * size,
            transcendentals=0,
        ),
        name="project",
    )(chunk, *terms, key_proj, value_proj)


def pieces_of(blocks, cuts):
    height = sum(cuts)
    starts = [sum(cuts[:c]) for c in range(len(cuts))]
    whole = blocks[0].shape[0] // height
    rows = [
        block[i * height + start : i * height + start + cut]
        for start, cut in zip(starts, cuts)
        for block in blocks
        for i in range(whole)
    ]
    count = len(blocks) * whole
    return jnp.concatenate(rows, 0), [(count * start, count * cut) for start, cut in zip(starts, cuts)]


def back_kernel(count, cuts, chunk_ref, *refs):
    states, downs, out_refs = refs[:count], refs[count : count + 2], refs[count + 2 :]
    size, _, hidden = out_refs[0].shape
    hidden = hidden // 2
    state, places = pieces_of([ref[...] for ref in states], cuts)
    for k in range(size):
        at = pl.ds(pl.multiple_of(chunk_ref[k] * hidden, hidden), hidden)
        for i in range(2):
            part = dot(state, downs[i][at, :], NT).astype(BF16)
            for (start, rows), out_ref in zip(places, out_refs):
                out_ref[k, :, i * hidden : (i + 1) * hidden] = part[start : start + rows]


def back_parts(chunk, states, downs, cuts):
    size, (height, width) = chunk.shape[0], states[0].shape
    count = len(states)
    if height % 16:
        states = [jnp.concatenate(states, 0)]
    hidden = downs[0].shape[0] // size
    return pl.pallas_call(
        functools.partial(back_kernel, len(states), cuts),
        in_specs=[pl.BlockSpec(memory_space=pltpu.SMEM)]
        + [pl.BlockSpec(memory_space=pltpu.VMEM)] * (len(states) + 2),
        out_shape=[jax.ShapeDtypeStruct((size, count * cut, 2 * hidden), BF16) for cut in cuts],
        compiler_params=pltpu.CompilerParams(vmem_limit_bytes=VMEM_BYTES),
        cost_estimate=pl.CostEstimate(
            flops=4 * count * height * width * hidden * size,
            bytes_accessed=4 * width * hidden * size,
            transcendentals=0,
        ),
        name="back",
    )(chunk, *states, *downs)


def pre_kernel(count, cuts, *refs):
    inputs, ups, out_refs = refs[:count], refs[count : count + 2], refs[len(refs) - len(cuts) :]
    hidden = out_refs[0].shape[1] // 2
    size = ups[0].shape[0]
    whole = [pieces_of([ref[k] for ref in inputs], cuts) for k in range(size)]
    for i in range(2):
        part = sum(dot(whole[k][0], ups[i][k, :hidden, :], NT) for k in range(size))
        for (start, rows), out_ref in zip(whole[0][1], out_refs):
            out_ref[:, i * hidden : (i + 1) * hidden] = part[start : start + rows]


def pre_parts(inputs, ups, hidden, cuts, after):
    count, height = len(inputs), inputs[0].shape[1]
    if height % 16:
        inputs = [jnp.concatenate(inputs, 1)]
    return pl.pallas_call(
        functools.partial(pre_kernel, len(inputs), cuts),
        in_specs=[pl.BlockSpec(x.shape, lambda: (0, 0, 0)) for x in (*inputs, *ups)]
        + [pl.BlockSpec(memory_space=pl.ANY)] * len(after),
        out_shape=[jax.ShapeDtypeStruct((count * cut, 2 * hidden), F32) for cut in cuts],
        compiler_params=pltpu.CompilerParams(vmem_limit_bytes=VMEM_BYTES),
        cost_estimate=pl.CostEstimate(
            flops=4 * count * height * hidden * ups[0].shape[0] * ups[0].shape[2],
            bytes_accessed=4 * ups[0].size,
            transcendentals=0,
        ),
        name="pre",
    )(*inputs, *ups, *after)


def feed_kernel(count, chunk_ref, *refs):
    terms, slope_ref, ups, out_ref = refs[:count], refs[count], refs[count + 1 : count + 3], refs[-1]
    back = sum(ref[...].astype(F32) for ref in terms)
    gated = (slope_ref[...] * back).astype(BF16)
    hidden = gated.shape[1] // 2
    size, _, width = ups[0].shape
    for k in range(size):
        part = sum(
            dot(gated[:, i * hidden : (i + 1) * hidden], ups[i][chunk_ref[k], :hidden, :], NN)
            for i in range(2)
        )
        out_ref[:, :, k * width : (k + 1) * width] = part.astype(BF16).reshape(
            out_ref.shape[0], out_ref.shape[1], width
        )


def feed(chunk, terms, slope, ups, blocks):
    rows = terms[0].shape[0]
    size, _, width = ups[0].shape
    hidden = terms[0].shape[1] // 2
    return pl.pallas_call(
        functools.partial(feed_kernel, len(terms)),
        in_specs=[pl.BlockSpec(memory_space=pltpu.SMEM)]
        + [pl.BlockSpec(memory_space=pltpu.VMEM)] * (len(terms) + 3),
        out_specs=pl.BlockSpec(memory_space=pltpu.VMEM),
        out_shape=jax.ShapeDtypeStruct((blocks, rows // blocks, size * width), BF16),
        compiler_params=pltpu.CompilerParams(vmem_limit_bytes=VMEM_BYTES),
        cost_estimate=pl.CostEstimate(
            flops=4 * rows * hidden * width * size,
            bytes_accessed=4 * hidden * width * size,
            transcendentals=0,
        ),
        name="feed",
    )(chunk, *terms, slope, *ups)


def local(queries, keys, values, out_grad, key_proj, value_proj, global_in, up_proj, down_proj):
    size, planes = lax.axis_size("seq"), lax.axis_size("heads")
    place = lax.axis_index("seq") ^ jnp.arange(size, dtype=jnp.int32)
    chunk = lax.axis_index("heads") ^ jnp.arange(planes, dtype=jnp.int32)
    far = size // 2
    rows, width = global_in.shape
    cuts = (rows,)

    downs = [down_proj, swap(down_proj, "seq", 1)]
    hidden = up_proj.shape[1] // planes
    own_up = lax.all_to_all(bundle(up_proj, global_in, planes), "heads", 0, 0)

    arrays = (queries, out_grad, keys, values)
    heads = queries.shape[1] // HD
    query_grad, even, odd = attend(place, *arrays, 0, heads)
    terms = scatter_rows([even], [odd], [])
    terms[0], downs[1] = lax.optimization_barrier((terms[0], downs[1]))
    near = prepare([value_proj], terms[:1])
    share = list(project(chunk, terms, key_proj, *near))
    own_up, share[0] = lax.optimization_barrier((own_up, share[0]))
    ups = [own_up, swap(own_up, "seq", 1)]
    shares = [share[0]] + [swap(share[k], "heads", k) for k in range(1, planes)]
    shares, ups[1] = lax.optimization_barrier((shares, ups[1]))
    state = sum(t.astype(F32) for t in shares)
    state_low = state.astype(BF16)
    inputs = gather_blocks(own_up[:, hidden:], "seq", 2, far)
    states = gather_blocks(state_low, "seq", 2, far)
    own_parts = back_parts(chunk, states[:1], downs, (rows,))
    parts = back_parts(chunk, states[1:], downs, cuts)
    inputs = gather_blocks(own_up[:, hidden:], "seq", 2, far)
    own_pre = pre_parts(inputs[:1], ups, hidden, (rows,), own_parts)
    pres = pre_parts(inputs[1:], ups, hidden, cuts, parts[:1])

    def grow(part, pre, blocks):
        terms = [part[0]] + [swap(part[k], "heads", k) for k in range(1, planes)]
        return feed(chunk, terms, slope_of(pre), ups, blocks)

    first_terms = [parts[0][0]] + [swap(parts[0][k], "heads", k) for k in range(1, planes)]
    own_part, first_terms[2] = lax.optimization_barrier((own_parts[0], first_terms[2]))
    first_grown = feed(chunk, first_terms, slope_of(pres[0]), ups, far - 1)
    own_grown = grow(own_part, own_pre[0], 1)[0]
    grads, start = [], 0
    for part, pre, cut in zip(parts, pres, cuts):
        grown = first_grown if start == 0 else grow(part, pre, far - 1)
        blocks = [own_grown[start : start + cut]] + [grown[j] for j in range(far - 1)]
        start += cut
        own = sum(t.astype(F32) for t in scatter_terms(blocks, "seq", 2))
        blocks = [own[:, k * width : (k + 1) * width] for k in range(planes)]
        grads.append(
            blocks[0]
            + sum(swap(blocks[k].astype(BF16), "heads", k).astype(F32) for k in range(1, planes))
        )
    global_grad = state + jnp.concatenate(grads, 0)
    return (query_grad, global_grad)


def solution(mesh):
    placed = (
        P("seq", "heads"),
        P(None, "heads"),
        P(None, "heads"),
        P("seq", "heads"),
        P(None, "heads"),
        P(None, "heads"),
        P("seq", "heads"),
        P("heads", "seq"),
        P("seq", "heads"),
    )
    return jax.shard_map(
        local,
        mesh=mesh,
        in_specs=placed,
        out_specs=(P("seq", "heads"), P("seq", "heads")),
        check_vma=False,
    )
```

```python
import functools
import math

import jax
import jax.numpy as jnp
from jax import lax
from jax.experimental import pallas as pl
from jax.experimental.pallas import tpu as pltpu
from jax.sharding import PartitionSpec as P

HD = 128
SCALE = HD**-0.5
SCALE_LOG2 = SCALE * math.log2(math.e)
BF16, F32 = jnp.bfloat16, jnp.float32
NT = (((1,), (1,)), ((), ()))
NN = (((1,), (0,)), ((), ()))
TN = (((0,), (0,)), ((), ()))
VMEM_BYTES = 24 * 2**20


def dot(a, b, dims):
    return lax.dot_general(a, b, dims, preferred_element_type=F32)


def slope_of(pre):
    return (
        0.5 * (1.0 + lax.erf(pre * 0.7071067811865476))
        + pre * jnp.exp(-0.5 * pre * pre) * 0.3989422804014327
    )


def swap(x, axis, distance):
    size = lax.axis_size(axis)
    return lax.ppermute(x, axis, [(i, i ^ distance) for i in range(size)])


def levels_of(first, count):
    levels = []
    while count > 1:
        radix = min(4, count)
        levels.append((first, radix))
        first, count = first * radix, count // radix
    return levels


def gather_blocks(x, axis, first, count):
    blocks = [x]
    for step, radix in levels_of(first, count):
        whole = blocks[0] if len(blocks) == 1 else jnp.stack(blocks)
        got = [swap(whole, axis, step * k) for k in range(1, radix)]
        for other in got:
            blocks = blocks + ([other] if whole is x else list(other))
    return blocks


def scatter_terms(blocks, axis, first, low=BF16):
    levels = levels_of(first, len(blocks))
    for step, radix in reversed(levels[1:]):
        span = step // first
        terms = [blocks[k * span : (k + 1) * span] for k in range(radix)]
        got = [swap(jnp.stack(terms[k]), axis, step * k) for k in range(1, radix)]
        blocks = [
            (terms[0][i].astype(F32) + sum(g[i].astype(F32) for g in got)).astype(low)
            for i in range(span)
        ]
    return [blocks[0]] + [swap(blocks[k], axis, first * k) for k in range(1, len(blocks))]


def attend_kernel(sub, place_ref, q_ref, g_ref, k_ref, v_ref, *rest):
    dq_ref, even_ref, odd_ref, acc_ref = rest[-4:]
    block = pl.program_id(1)
    keys, values = k_ref[...], v_ref[...]

    @pl.when(block == 0)
    def _():
        acc_ref[...] = jnp.zeros_like(acc_ref)

    def products(at):
        return dot(keys, q_ref[at, :], NT), dot(values, g_ref[at, :], NT)

    def soften(scores, weight_grad):
        top = jnp.max(scores, axis=0, keepdims=True)
        grown = jnp.exp2((scores - top) * SCALE_LOG2)
        weights = grown * (1.0 / jnp.sum(grown, axis=0, keepdims=True))
        centre = jnp.sum(weights * weight_grad, axis=0, keepdims=True)
        return (weights * (weight_grad - centre)).astype(BF16), weights.astype(BF16)

    def collect(at, score_grad, weights_low):
        dq_ref[at, :] = (SCALE * dot(keys, score_grad, TN)).T.astype(BF16)
        acc_ref[:, :HD] += dot(score_grad, q_ref[at, :], NN)
        acc_ref[:, HD:] += dot(weights_low, g_ref[at, :], NN)

    pieces = [pl.ds(i * sub, sub) for i in range(q_ref.shape[0] // sub)]
    ahead, behind = products(pieces[0]), None
    for i, at in enumerate(pieces):
        now, ahead = ahead, products(pieces[i + 1]) if i + 1 < len(pieces) else None
        if behind is not None:
            collect(pieces[i - 1], *behind)
        behind = soften(*now)
    collect(pieces[-1], *behind)

    @pl.when(block == pl.num_programs(1) - 1)
    def _():
        acc_ref[:, :HD] = SCALE * acc_ref[:, :HD]
        half, height = even_ref.shape[:2]
        for j in range(2 * half):
            at = pl.ds(pl.multiple_of(place_ref[j] * height, height), height)
            (odd_ref if j % 2 else even_ref)[j // 2] = acc_ref[at, :].astype(BF16)


def attend(place, queries, out_grad, keys, values, first, count, query_grad=None, after=()):
    tokens, width = queries.shape
    glob, size = keys.shape[0], place.shape[0]
    block = min(2048, tokens)
    token_spec = pl.BlockSpec((block, HD), lambda h, b, place: (b, h + first))
    global_spec = pl.BlockSpec((glob, HD), lambda h, b, place: (0, h + first))
    part_spec = pl.BlockSpec((size // 2, glob // size, 2 * HD), lambda h, b, place: (0, 0, h))
    part = pltpu.VMEM((size // 2, glob // size, 2 * HD * count), BF16)
    extra = [x for x in (query_grad, *after) if x is not None]
    return pl.pallas_call(
        functools.partial(attend_kernel, min(256, block)),
        grid_spec=pltpu.PrefetchScalarGridSpec(
            num_scalar_prefetch=1,
            grid=(count, tokens // block),
            in_specs=[token_spec, token_spec, global_spec, global_spec]
            + [pl.BlockSpec(memory_space=pl.ANY)] * len(extra),
            out_specs=[token_spec, part_spec, part_spec],
            scratch_shapes=[pltpu.VMEM((glob, 2 * HD), F32)],
        ),
        out_shape=[pltpu.HBM((tokens, width), BF16), part, part],
        input_output_aliases={} if query_grad is None else {5: 0},
        compiler_params=pltpu.CompilerParams(vmem_limit_bytes=VMEM_BYTES),
        cost_estimate=pl.CostEstimate(
            flops=20 * tokens * glob * HD * count,
            bytes_accessed=6 * tokens * HD * count,
            transcendentals=tokens * glob * count,
        ),
        name="attend",
    )(place, *map(hold, (queries, out_grad, keys, values)), *extra)


def hold(x):
    return pltpu.with_memory_space_constraint(x, pltpu.HBM)


def bundle_kernel(up_ref, in_ref, out_ref):
    size, depth, _ = out_ref.shape
    rows = in_ref.shape[0]
    hidden = depth - rows
    for k in range(size):
        out_ref[k, :hidden, :] = up_ref[:, k * hidden : (k + 1) * hidden].T
        out_ref[k, hidden:, :] = in_ref[...]


def bundle(up_proj, global_in, size):
    (width, hidden), rows = up_proj.shape, global_in.shape[0]
    if (hidden // size) % 128 or rows % 16:
        return jnp.concatenate(
            [
                up_proj.T.reshape(size, hidden // size, width),
                jnp.broadcast_to(global_in[None], (size, rows, width)),
            ],
            1,
        )
    return pl.pallas_call(
        bundle_kernel,
        out_shape=jax.ShapeDtypeStruct((size, hidden // size + rows, width), BF16),
        compiler_params=pltpu.CompilerParams(vmem_limit_bytes=VMEM_BYTES),
        cost_estimate=pl.CostEstimate(
            flops=0, bytes_accessed=4 * up_proj.size, transcendentals=0
        ),
        name="bundle",
    )(hold(up_proj), hold(global_in))


def merge_kernel(count, *refs):
    evens, gots = refs[:count], refs[count : 2 * count]
    out_refs = refs[len(refs) - evens[0].shape[0] :]
    at = 0
    for even_ref, got_ref in zip(evens, gots):
        cols = pl.ds(at, even_ref.shape[2])
        at += even_ref.shape[2]
        for j, out_ref in enumerate(out_refs):
            out_ref[:, cols] = (even_ref[j].astype(F32) + got_ref[j].astype(F32)).astype(BF16)


def scatter_rows(evens, odds, near):
    gots = [swap(odd, "seq", 1) for odd in odds]
    blocks, rows, _ = evens[0].shape
    width = sum(even.shape[2] for even in evens)
    spec = lambda x: pl.BlockSpec(x.shape, lambda: (0, 0, 0))
    mine = pl.pallas_call(
        functools.partial(merge_kernel, len(evens)),
        in_specs=[spec(x) for x in (*evens, *gots)]
        + [pl.BlockSpec(memory_space=pltpu.VMEM)] * len(near),
        out_shape=[pltpu.VMEM((rows, width), BF16)] * blocks,
        compiler_params=pltpu.CompilerParams(vmem_limit_bytes=VMEM_BYTES),
        cost_estimate=pl.CostEstimate(
            flops=blocks * rows * width, bytes_accessed=6 * blocks * rows * width, transcendentals=0
        ),
        name="merge",
    )(*evens, *gots, *near)
    return scatter_terms(mine, "seq", 2)


def prepare_kernel(*refs):
    half = len(refs) // 2
    for from_ref, to_ref in zip(refs[:half], refs[half:]):
        to_ref[...] = from_ref[...].T


def prepare(arrays, after):
    count = len(arrays)
    return pl.pallas_call(
        lambda *refs: prepare_kernel(*refs[:count], *refs[count + len(after) :]),
        grid=(4,),
        in_specs=[pl.BlockSpec((x.shape[0] // 4, x.shape[1]), lambda i: (i, 0)) for x in arrays]
        + [pl.BlockSpec(memory_space=pl.ANY)] * len(after),
        out_specs=[pl.BlockSpec((x.shape[1], x.shape[0] // 4), lambda i: (0, i)) for x in arrays],
        out_shape=[pltpu.VMEM(x.shape[::-1], x.dtype) for x in arrays],
        compiler_params=pltpu.CompilerParams(vmem_limit_bytes=VMEM_BYTES),
        cost_estimate=pl.CostEstimate(
            flops=0, bytes_accessed=4 * arrays[0].size, transcendentals=0
        ),
        name="prepare",
    )(*map(hold, arrays), *after)


def project_kernel(count, chunk_ref, *refs):
    terms, (key_proj_ref, value_proj_ref) = refs[:count], refs[count : count + 2]
    part_refs = refs[count + 2 :]
    total = sum(t[...].astype(F32) for t in terms).astype(BF16)
    heads = total.shape[1] // (2 * HD)
    pick = lambda at: [total[:, (2 * h + at) * HD : (2 * h + at + 1) * HD] for h in range(heads)]
    key_low, value_low = jnp.concatenate(pick(0), 1), jnp.concatenate(pick(1), 1)
    block = part_refs[0].shape[1]
    for k, part_ref in enumerate(part_refs):
        at = pl.ds(pl.multiple_of(chunk_ref[k] * block, block), block)
        part = dot(key_low, key_proj_ref[:, at], NN) + dot(value_low, value_proj_ref[:, at], NN)
        part_ref[...] = part.astype(BF16)


def project(chunk, terms, key_proj, value_proj):
    rows, width = terms[0].shape
    size = chunk.shape[0]
    block = key_proj.shape[1] // size
    part = pltpu.HBM((rows, block), BF16)
    return pl.pallas_call(
        functools.partial(project_kernel, len(terms)),
        in_specs=[pl.BlockSpec(memory_space=pltpu.SMEM)]
        + [pl.BlockSpec(memory_space=pltpu.VMEM)] * (len(terms) + 2),
        out_specs=[pl.BlockSpec((rows, block), lambda: (0, 0))] * size,
        out_shape=[part] * size,
        compiler_params=pltpu.CompilerParams(vmem_limit_bytes=VMEM_BYTES),
        cost_estimate=pl.CostEstimate(
            flops=2 * rows * width * block * size,
            bytes_accessed=2 * width * block * size,
            transcendentals=0,
        ),
        name="project",
    )(chunk, *terms, key_proj, value_proj)


def pieces_of(blocks, cuts):
    height = sum(cuts)
    starts = [sum(cuts[:c]) for c in range(len(cuts))]
    whole = blocks[0].shape[0] // height
    rows = [
        block[i * height + start : i * height + start + cut]
        for start, cut in zip(starts, cuts)
        for block in blocks
        for i in range(whole)
    ]
    count = len(blocks) * whole
    return jnp.concatenate(rows, 0), [(count * start, count * cut) for start, cut in zip(starts, cuts)]


def back_kernel(count, cuts, chunk_ref, *refs):
    states, downs, out_refs = refs[:count], refs[count : count + 2], refs[count + 2 :]
    size, _, hidden = out_refs[0].shape
    hidden = hidden // 2
    state, places = pieces_of([ref[...] for ref in states], cuts)
    for k in range(size):
        at = pl.ds(pl.multiple_of(chunk_ref[k] * hidden, hidden), hidden)
        for i in range(2):
            part = dot(state, downs[i][at, :], NT).astype(BF16)
            for (start, rows), out_ref in zip(places, out_refs):
                out_ref[k, :, i * hidden : (i + 1) * hidden] = part[start : start + rows]


def back_parts(chunk, states, downs, cuts):
    size, (height, width) = chunk.shape[0], states[0].shape
    count = len(states)
    if height % 16:
        states = [jnp.concatenate(states, 0)]
    hidden = downs[0].shape[0] // size
    return pl.pallas_call(
        functools.partial(back_kernel, len(states), cuts),
        in_specs=[pl.BlockSpec(memory_space=pltpu.SMEM)]
        + [pl.BlockSpec(memory_space=pltpu.VMEM)] * (len(states) + 2),
        out_shape=[jax.ShapeDtypeStruct((size, count * cut, 2 * hidden), BF16) for cut in cuts],
        compiler_params=pltpu.CompilerParams(vmem_limit_bytes=VMEM_BYTES),
        cost_estimate=pl.CostEstimate(
            flops=4 * count * height * width * hidden * size,
            bytes_accessed=4 * width * hidden * size,
            transcendentals=0,
        ),
        name="back",
    )(chunk, *states, *downs)


def pre_kernel(count, cuts, *refs):
    inputs, ups, out_refs = refs[:count], refs[count : count + 2], refs[len(refs) - len(cuts) :]
    hidden = out_refs[0].shape[1] // 2
    size = ups[0].shape[0]
    whole = [pieces_of([ref[k] for ref in inputs], cuts) for k in range(size)]
    for i in range(2):
        part = sum(dot(whole[k][0], ups[i][k, :hidden, :], NT) for k in range(size))
        for (start, rows), out_ref in zip(whole[0][1], out_refs):
            out_ref[:, i * hidden : (i + 1) * hidden] = part[start : start + rows]


def pre_parts(inputs, ups, hidden, cuts, after):
    count, height = len(inputs), inputs[0].shape[1]
    if height % 16:
        inputs = [jnp.concatenate(inputs, 1)]
    return pl.pallas_call(
        functools.partial(pre_kernel, len(inputs), cuts),
        in_specs=[pl.BlockSpec(x.shape, lambda: (0, 0, 0)) for x in (*inputs, *ups)]
        + [pl.BlockSpec(memory_space=pl.ANY)] * len(after),
        out_shape=[jax.ShapeDtypeStruct((count * cut, 2 * hidden), F32) for cut in cuts],
        compiler_params=pltpu.CompilerParams(vmem_limit_bytes=VMEM_BYTES),
        cost_estimate=pl.CostEstimate(
            flops=4 * count * height * hidden * ups[0].shape[0] * ups[0].shape[2],
            bytes_accessed=4 * ups[0].size,
            transcendentals=0,
        ),
        name="pre",
    )(*inputs, *ups, *after)


def feed_kernel(count, chunk_ref, *refs):
    terms, slope_ref, ups, out_ref = refs[:count], refs[count], refs[count + 1 : count + 3], refs[-1]
    back = sum(ref[...].astype(F32) for ref in terms)
    gated = (slope_ref[...] * back).astype(BF16)
    hidden = gated.shape[1] // 2
    size, _, width = ups[0].shape
    for k in range(size):
        part = sum(
            dot(gated[:, i * hidden : (i + 1) * hidden], ups[i][chunk_ref[k], :hidden, :], NN)
            for i in range(2)
        )
        out_ref[:, :, k * width : (k + 1) * width] = part.astype(BF16).reshape(
            out_ref.shape[0], out_ref.shape[1], width
        )


def feed(chunk, terms, slope, ups, blocks):
    rows = terms[0].shape[0]
    size, _, width = ups[0].shape
    hidden = terms[0].shape[1] // 2
    return pl.pallas_call(
        functools.partial(feed_kernel, len(terms)),
        in_specs=[pl.BlockSpec(memory_space=pltpu.SMEM)]
        + [pl.BlockSpec(memory_space=pltpu.VMEM)] * (len(terms) + 3),
        out_specs=pl.BlockSpec(memory_space=pltpu.VMEM),
        out_shape=jax.ShapeDtypeStruct((blocks, rows // blocks, size * width), BF16),
        compiler_params=pltpu.CompilerParams(vmem_limit_bytes=VMEM_BYTES),
        cost_estimate=pl.CostEstimate(
            flops=4 * rows * hidden * width * size,
            bytes_accessed=4 * hidden * width * size,
            transcendentals=0,
        ),
        name="feed",
    )(chunk, *terms, slope, *ups)


def local(queries, keys, values, out_grad, key_proj, value_proj, global_in, up_proj, down_proj):
    size, planes = lax.axis_size("seq"), lax.axis_size("heads")
    place = lax.axis_index("seq") ^ jnp.arange(size, dtype=jnp.int32)
    chunk = lax.axis_index("heads") ^ jnp.arange(planes, dtype=jnp.int32)
    far = size // 2
    rows, width = global_in.shape
    cuts = (rows,)

    downs = [down_proj, swap(down_proj, "seq", 1)]
    hidden = up_proj.shape[1] // planes
    own_up = lax.all_to_all(bundle(up_proj, global_in, planes), "heads", 0, 0)

    arrays = (queries, out_grad, keys, values)
    heads = queries.shape[1] // HD
    query_grad, even, odd = attend(place, *arrays, 0, heads)
    terms = scatter_rows([even], [odd], [])
    terms[0], downs[1] = lax.optimization_barrier((terms[0], downs[1]))
    near = prepare([key_proj, value_proj], terms[:1])
    share = list(project(chunk, terms, *near))
    own_up, share[0] = lax.optimization_barrier((own_up, share[0]))
    ups = [own_up, swap(own_up, "seq", 1)]
    shares = [share[0]] + [swap(share[k], "heads", k) for k in range(1, planes)]
    shares, ups[1] = lax.optimization_barrier((shares, ups[1]))
    state = sum(t.astype(F32) for t in shares)
    state_low = state.astype(BF16)
    inputs = gather_blocks(own_up[:, hidden:], "seq", 2, far)
    states = gather_blocks(state_low, "seq", 2, far)
    own_parts = back_parts(chunk, states[:1], downs, (rows,))
    parts = back_parts(chunk, states[1:], downs, cuts)
    inputs = gather_blocks(own_up[:, hidden:], "seq", 2, far)
    own_pre = pre_parts(inputs[:1], ups, hidden, (rows,), own_parts)
    pres = pre_parts(inputs[1:], ups, hidden, cuts, parts[:1])

    def grow(part, pre, blocks):
        terms = [part[0]] + [swap(part[k], "heads", k) for k in range(1, planes)]
        return feed(chunk, terms, slope_of(pre), ups, blocks)

    first_terms = [parts[0][0]] + [swap(parts[0][k], "heads", k) for k in range(1, planes)]
    own_part, first_terms[2] = lax.optimization_barrier((own_parts[0], first_terms[2]))
    first_grown = feed(chunk, first_terms, slope_of(pres[0]), ups, far - 1)
    own_grown = grow(own_part, own_pre[0], 1)[0]
    grads, start = [], 0
    for part, pre, cut in zip(parts, pres, cuts):
        grown = first_grown if start == 0 else grow(part, pre, far - 1)
        blocks = [own_grown[start : start + cut]] + [grown[j] for j in range(far - 1)]
        start += cut
        own = sum(t.astype(F32) for t in scatter_terms(blocks, "seq", 2))
        blocks = [own[:, k * width : (k + 1) * width] for k in range(planes)]
        grads.append(
            blocks[0]
            + sum(swap(blocks[k].astype(BF16), "heads", k).astype(F32) for k in range(1, planes))
        )
    global_grad = state + jnp.concatenate(grads, 0)
    return (query_grad, global_grad)


def solution(mesh):
    placed = (
        P("seq", "heads"),
        P(None, "heads"),
        P(None, "heads"),
        P("seq", "heads"),
        P(None, "heads"),
        P(None, "heads"),
        P("seq", "heads"),
        P("heads", "seq"),
        P("seq", "heads"),
    )
    return jax.shard_map(
        local,
        mesh=mesh,
        in_specs=placed,
        out_specs=(P("seq", "heads"), P("seq", "heads")),
        check_vma=False,
    )
```

```python
import functools
import math

import jax
import jax.numpy as jnp
from jax import lax
from jax.experimental import pallas as pl
from jax.experimental.pallas import tpu as pltpu
from jax.sharding import PartitionSpec as P

HD = 128
SCALE = HD**-0.5
SCALE_LOG2 = SCALE * math.log2(math.e)
BF16, F32 = jnp.bfloat16, jnp.float32
NT = (((1,), (1,)), ((), ()))
NN = (((1,), (0,)), ((), ()))
TN = (((0,), (0,)), ((), ()))
VMEM_BYTES = 24 * 2**20


def dot(a, b, dims):
    return lax.dot_general(a, b, dims, preferred_element_type=F32)


def slope_of(pre):
    return (
        0.5 * (1.0 + lax.erf(pre * 0.7071067811865476))
        + pre * jnp.exp(-0.5 * pre * pre) * 0.3989422804014327
    )


def swap(x, axis, distance):
    size = lax.axis_size(axis)
    return lax.ppermute(x, axis, [(i, i ^ distance) for i in range(size)])


def levels_of(first, count):
    levels = []
    while count > 1:
        radix = min(4, count)
        levels.append((first, radix))
        first, count = first * radix, count // radix
    return levels


def gather_blocks(x, axis, first, count):
    blocks = [x]
    for step, radix in levels_of(first, count):
        whole = blocks[0] if len(blocks) == 1 else jnp.stack(blocks)
        got = [swap(whole, axis, step * k) for k in range(1, radix)]
        for other in got:
            blocks = blocks + ([other] if whole is x else list(other))
    return blocks


def scatter_terms(blocks, axis, first, low=BF16):
    levels = levels_of(first, len(blocks))
    for step, radix in reversed(levels[1:]):
        span = step // first
        terms = [blocks[k * span : (k + 1) * span] for k in range(radix)]
        got = [swap(jnp.stack(terms[k]), axis, step * k) for k in range(1, radix)]
        blocks = [
            (terms[0][i].astype(F32) + sum(g[i].astype(F32) for g in got)).astype(low)
            for i in range(span)
        ]
    return [blocks[0]] + [swap(blocks[k], axis, first * k) for k in range(1, len(blocks))]


def attend_kernel(sub, place_ref, q_ref, g_ref, k_ref, v_ref, *rest):
    dq_ref, even_ref, odd_ref, acc_ref = rest[-4:]
    block = pl.program_id(1)
    keys, values = k_ref[...], v_ref[...]

    @pl.when(block == 0)
    def _():
        acc_ref[...] = jnp.zeros_like(acc_ref)

    def products(at):
        return dot(keys, q_ref[at, :], NT), dot(values, g_ref[at, :], NT)

    def soften(scores, weight_grad):
        top = jnp.max(scores, axis=0, keepdims=True)
        grown = jnp.exp2((scores - top) * SCALE_LOG2)
        weights = grown * (1.0 / jnp.sum(grown, axis=0, keepdims=True))
        centre = jnp.sum(weights * weight_grad, axis=0, keepdims=True)
        return (weights * (weight_grad - centre)).astype(BF16), weights.astype(BF16)

    def collect(at, score_grad, weights_low):
        dq_ref[at, :] = (SCALE * dot(keys, score_grad, TN)).T.astype(BF16)
        acc_ref[:, :HD] += dot(score_grad, q_ref[at, :], NN)
        acc_ref[:, HD:] += dot(weights_low, g_ref[at, :], NN)

    pieces = [pl.ds(i * sub, sub) for i in range(q_ref.shape[0] // sub)]
    ahead, behind = products(pieces[0]), None
    for i, at in enumerate(pieces):
        now, ahead = ahead, products(pieces[i + 1]) if i + 1 < len(pieces) else None
        if behind is not None:
            collect(pieces[i - 1], *behind)
        behind = soften(*now)
    collect(pieces[-1], *behind)

    @pl.when(block == pl.num_programs(1) - 1)
    def _():
        acc_ref[:, :HD] = SCALE * acc_ref[:, :HD]
        half, height = even_ref.shape[:2]
        for j in range(2 * half):
            at = pl.ds(pl.multiple_of(place_ref[j] * height, height), height)
            (odd_ref if j % 2 else even_ref)[j // 2] = acc_ref[at, :].astype(BF16)


def attend(place, queries, out_grad, keys, values, first, count, query_grad=None, after=()):
    tokens, width = queries.shape
    glob, size = keys.shape[0], place.shape[0]
    block = min(2048, tokens)
    token_spec = pl.BlockSpec((block, HD), lambda h, b, place: (b, h + first))
    global_spec = pl.BlockSpec((glob, HD), lambda h, b, place: (0, h + first))
    part_spec = pl.BlockSpec((size // 2, glob // size, 2 * HD), lambda h, b, place: (0, 0, h))
    part = pltpu.VMEM((size // 2, glob // size, 2 * HD * count), BF16)
    extra = [x for x in (query_grad, *after) if x is not None]
    return pl.pallas_call(
        functools.partial(attend_kernel, min(256, block)),
        grid_spec=pltpu.PrefetchScalarGridSpec(
            num_scalar_prefetch=1,
            grid=(count, tokens // block),
            in_specs=[token_spec, token_spec, global_spec, global_spec]
            + [pl.BlockSpec(memory_space=pl.ANY)] * len(extra),
            out_specs=[token_spec, part_spec, part_spec],
            scratch_shapes=[pltpu.VMEM((glob, 2 * HD), F32)],
        ),
        out_shape=[pltpu.HBM((tokens, width), BF16), part, part],
        input_output_aliases={} if query_grad is None else {5: 0},
        compiler_params=pltpu.CompilerParams(vmem_limit_bytes=VMEM_BYTES),
        cost_estimate=pl.CostEstimate(
            flops=20 * tokens * glob * HD * count,
            bytes_accessed=6 * tokens * HD * count,
            transcendentals=tokens * glob * count,
        ),
        name="attend",
    )(place, *map(hold, (queries, out_grad, keys, values)), *extra)


def hold(x):
    return pltpu.with_memory_space_constraint(x, pltpu.HBM)


def bundle_kernel(up_ref, in_ref, out_ref):
    size, depth, _ = out_ref.shape
    rows = in_ref.shape[0]
    hidden = depth - rows
    for k in range(size):
        out_ref[k, :hidden, :] = up_ref[:, k * hidden : (k + 1) * hidden].T
        out_ref[k, hidden:, :] = in_ref[...]


def bundle(up_proj, global_in, size):
    (width, hidden), rows = up_proj.shape, global_in.shape[0]
    if (hidden // size) % 128 or rows % 16:
        return jnp.concatenate(
            [
                up_proj.T.reshape(size, hidden // size, width),
                jnp.broadcast_to(global_in[None], (size, rows, width)),
            ],
            1,
        )
    return pl.pallas_call(
        bundle_kernel,
        out_shape=jax.ShapeDtypeStruct((size, hidden // size + rows, width), BF16),
        compiler_params=pltpu.CompilerParams(vmem_limit_bytes=VMEM_BYTES),
        cost_estimate=pl.CostEstimate(
            flops=0, bytes_accessed=4 * up_proj.size, transcendentals=0
        ),
        name="bundle",
    )(hold(up_proj), hold(global_in))


def merge_kernel(count, *refs):
    evens, gots = refs[:count], refs[count : 2 * count]
    out_refs = refs[len(refs) - evens[0].shape[0] :]
    at = 0
    for even_ref, got_ref in zip(evens, gots):
        cols = pl.ds(at, even_ref.shape[2])
        at += even_ref.shape[2]
        for j, out_ref in enumerate(out_refs):
            out_ref[:, cols] = (even_ref[j].astype(F32) + got_ref[j].astype(F32)).astype(BF16)


def scatter_rows(evens, odds, near):
    gots = [swap(odd, "seq", 1) for odd in odds]
    blocks, rows, _ = evens[0].shape
    width = sum(even.shape[2] for even in evens)
    spec = lambda x: pl.BlockSpec(x.shape, lambda: (0, 0, 0))
    mine = pl.pallas_call(
        functools.partial(merge_kernel, len(evens)),
        in_specs=[spec(x) for x in (*evens, *gots)]
        + [pl.BlockSpec(memory_space=pltpu.VMEM)] * len(near),
        out_shape=[pltpu.VMEM((rows, width), BF16)] * blocks,
        compiler_params=pltpu.CompilerParams(vmem_limit_bytes=VMEM_BYTES),
        cost_estimate=pl.CostEstimate(
            flops=blocks * rows * width, bytes_accessed=6 * blocks * rows * width, transcendentals=0
        ),
        name="merge",
    )(*evens, *gots, *near)
    return scatter_terms(mine, "seq", 2)


def prepare_kernel(*refs):
    half = len(refs) // 2
    for from_ref, to_ref in zip(refs[:half], refs[half:]):
        to_ref[...] = from_ref[...].T


def prepare(arrays, after):
    count = len(arrays)
    return pl.pallas_call(
        lambda *refs: prepare_kernel(*refs[:count], *refs[count + len(after) :]),
        grid=(4,),
        in_specs=[pl.BlockSpec((x.shape[0] // 4, x.shape[1]), lambda i: (i, 0)) for x in arrays]
        + [pl.BlockSpec(memory_space=pl.ANY)] * len(after),
        out_specs=[pl.BlockSpec((x.shape[1], x.shape[0] // 4), lambda i: (0, i)) for x in arrays],
        out_shape=[pltpu.VMEM(x.shape[::-1], x.dtype) for x in arrays],
        compiler_params=pltpu.CompilerParams(vmem_limit_bytes=VMEM_BYTES),
        cost_estimate=pl.CostEstimate(
            flops=0, bytes_accessed=4 * arrays[0].size, transcendentals=0
        ),
        name="prepare",
    )(*map(hold, arrays), *after)


def project_kernel(count, chunk_ref, *refs):
    terms, (key_proj_ref, value_proj_ref) = refs[:count], refs[count : count + 2]
    part_refs = refs[count + 2 :]
    total = sum(t[...].astype(F32) for t in terms).astype(BF16)
    heads = total.shape[1] // (2 * HD)
    pick = lambda at: [total[:, (2 * h + at) * HD : (2 * h + at + 1) * HD] for h in range(heads)]
    key_low, value_low = jnp.concatenate(pick(0), 1), jnp.concatenate(pick(1), 1)
    block = part_refs[0].shape[1]
    for k, part_ref in enumerate(part_refs):
        at = pl.ds(pl.multiple_of(chunk_ref[k] * block, block), block)
        part = dot(key_low, key_proj_ref[:, at], NN) + dot(value_low, value_proj_ref[:, at], NN)
        part_ref[...] = part.astype(BF16)


def project(chunk, terms, key_proj, value_proj):
    rows, width = terms[0].shape
    size = chunk.shape[0]
    block = key_proj.shape[1] // size
    part = pltpu.HBM((rows, block), BF16)
    return pl.pallas_call(
        functools.partial(project_kernel, len(terms)),
        in_specs=[pl.BlockSpec(memory_space=pltpu.SMEM)]
        + [pl.BlockSpec(memory_space=pltpu.VMEM)] * (len(terms) + 2),
        out_specs=[pl.BlockSpec((rows, block), lambda: (0, 0))] * size,
        out_shape=[part] * size,
        compiler_params=pltpu.CompilerParams(vmem_limit_bytes=VMEM_BYTES),
        cost_estimate=pl.CostEstimate(
            flops=2 * rows * width * block * size,
            bytes_accessed=2 * width * block * size,
            transcendentals=0,
        ),
        name="project",
    )(chunk, *terms, key_proj, value_proj)


def pieces_of(blocks, cuts):
    height = sum(cuts)
    starts = [sum(cuts[:c]) for c in range(len(cuts))]
    whole = blocks[0].shape[0] // height
    rows = [
        block[i * height + start : i * height + start + cut]
        for start, cut in zip(starts, cuts)
        for block in blocks
        for i in range(whole)
    ]
    count = len(blocks) * whole
    return jnp.concatenate(rows, 0), [(count * start, count * cut) for start, cut in zip(starts, cuts)]


def back_kernel(count, cuts, chunk_ref, *refs):
    states, downs, out_refs = refs[:count], refs[count : count + 2], refs[count + 2 :]
    size, _, hidden = out_refs[0].shape
    hidden = hidden // 2
    state, places = pieces_of([ref[...] for ref in states], cuts)
    for k in range(size):
        at = pl.ds(pl.multiple_of(chunk_ref[k] * hidden, hidden), hidden)
        for i in range(2):
            part = dot(state, downs[i][at, :], NT).astype(BF16)
            for (start, rows), out_ref in zip(places, out_refs):
                out_ref[k, :, i * hidden : (i + 1) * hidden] = part[start : start + rows]


def back_parts(chunk, states, downs, cuts):
    size, (height, width) = chunk.shape[0], states[0].shape
    count = len(states)
    if height % 16:
        states = [jnp.concatenate(states, 0)]
    hidden = downs[0].shape[0] // size
    return pl.pallas_call(
        functools.partial(back_kernel, len(states), cuts),
        in_specs=[pl.BlockSpec(memory_space=pltpu.SMEM)]
        + [pl.BlockSpec(memory_space=pltpu.VMEM)] * (len(states) + 2),
        out_shape=[jax.ShapeDtypeStruct((size, count * cut, 2 * hidden), BF16) for cut in cuts],
        compiler_params=pltpu.CompilerParams(vmem_limit_bytes=VMEM_BYTES),
        cost_estimate=pl.CostEstimate(
            flops=4 * count * height * width * hidden * size,
            bytes_accessed=4 * width * hidden * size,
            transcendentals=0,
        ),
        name="back",
    )(chunk, *states, *downs)


def pre_kernel(count, cuts, *refs):
    inputs, ups, out_refs = refs[:count], refs[count : count + 2], refs[len(refs) - len(cuts) :]
    hidden = out_refs[0].shape[1] // 2
    size = ups[0].shape[0]
    whole = [pieces_of([ref[k] for ref in inputs], cuts) for k in range(size)]
    for i in range(2):
        part = sum(dot(whole[k][0], ups[i][k, :hidden, :], NT) for k in range(size))
        for (start, rows), out_ref in zip(whole[0][1], out_refs):
            out_ref[:, i * hidden : (i + 1) * hidden] = part[start : start + rows]


def pre_parts(inputs, ups, hidden, cuts, after):
    count, height = len(inputs), inputs[0].shape[1]
    if height % 16:
        inputs = [jnp.concatenate(inputs, 1)]
    return pl.pallas_call(
        functools.partial(pre_kernel, len(inputs), cuts),
        in_specs=[pl.BlockSpec(x.shape, lambda: (0, 0, 0)) for x in (*inputs, *ups)]
        + [pl.BlockSpec(memory_space=pl.ANY)] * len(after),
        out_shape=[jax.ShapeDtypeStruct((count * cut, 2 * hidden), F32) for cut in cuts],
        compiler_params=pltpu.CompilerParams(vmem_limit_bytes=VMEM_BYTES),
        cost_estimate=pl.CostEstimate(
            flops=4 * count * height * hidden * ups[0].shape[0] * ups[0].shape[2],
            bytes_accessed=4 * ups[0].size,
            transcendentals=0,
        ),
        name="pre",
    )(*inputs, *ups, *after)


def feed_kernel(count, chunk_ref, *refs):
    terms, slope_ref, ups, out_ref = refs[:count], refs[count], refs[count + 1 : count + 3], refs[-1]
    back = sum(ref[...].astype(F32) for ref in terms)
    gated = (slope_ref[...] * back).astype(BF16)
    hidden = gated.shape[1] // 2
    size, _, width = ups[0].shape
    for k in range(size):
        part = sum(
            dot(gated[:, i * hidden : (i + 1) * hidden], ups[i][chunk_ref[k], :hidden, :], NN)
            for i in range(2)
        )
        out_ref[:, :, k * width : (k + 1) * width] = part.astype(BF16).reshape(
            out_ref.shape[0], out_ref.shape[1], width
        )


def feed(chunk, terms, slope, ups, blocks):
    rows = terms[0].shape[0]
    size, _, width = ups[0].shape
    hidden = terms[0].shape[1] // 2
    return pl.pallas_call(
        functools.partial(feed_kernel, len(terms)),
        in_specs=[pl.BlockSpec(memory_space=pltpu.SMEM)]
        + [pl.BlockSpec(memory_space=pltpu.VMEM)] * (len(terms) + 3),
        out_specs=pl.BlockSpec(memory_space=pltpu.VMEM),
        out_shape=jax.ShapeDtypeStruct((blocks, rows // blocks, size * width), BF16),
        compiler_params=pltpu.CompilerParams(vmem_limit_bytes=VMEM_BYTES),
        cost_estimate=pl.CostEstimate(
            flops=4 * rows * hidden * width * size,
            bytes_accessed=4 * hidden * width * size,
            transcendentals=0,
        ),
        name="feed",
    )(chunk, *terms, slope, *ups)


def local(queries, keys, values, out_grad, key_proj, value_proj, global_in, up_proj, down_proj):
    size, planes = lax.axis_size("seq"), lax.axis_size("heads")
    place = lax.axis_index("seq") ^ jnp.arange(size, dtype=jnp.int32)
    chunk = lax.axis_index("heads") ^ jnp.arange(planes, dtype=jnp.int32)
    far = size // 2
    rows, width = global_in.shape
    cuts = (rows,)

    downs = [down_proj, swap(down_proj, "seq", 1)]
    hidden = up_proj.shape[1] // planes
    own_up = lax.all_to_all(bundle(up_proj, global_in, planes), "heads", 0, 0)

    arrays = (queries, out_grad, keys, values)
    heads = queries.shape[1] // HD
    query_grad, even, odd = attend(place, *arrays, 0, heads)
    terms = scatter_rows([even], [odd], [])
    terms[0], downs[1] = lax.optimization_barrier((terms[0], downs[1]))
    near = prepare([key_proj, value_proj], terms[:1])
    share = list(project(chunk, terms, *near))
    own_up, share[0] = lax.optimization_barrier((own_up, share[0]))
    ups = [own_up, swap(own_up, "seq", 1)]
    shares = [share[0]] + [swap(share[k], "heads", k) for k in range(1, planes)]
    shares, ups[1] = lax.optimization_barrier((shares, ups[1]))
    state = sum(t.astype(F32) for t in shares)
    state_low = state.astype(BF16)
    inputs = gather_blocks(own_up[:, hidden:], "seq", 2, far)
    states = gather_blocks(state_low, "seq", 2, far)
    own_parts = back_parts(chunk, states[:1], downs, (rows,))
    parts = back_parts(chunk, states[1:], downs, cuts)
    inputs = gather_blocks(own_up[:, hidden:], "seq", 2, far)
    pre = pre_parts(inputs, ups, hidden, cuts, parts[:1])[0]
    own_pre, pres = [pre[:rows]], [pre[rows:]]

    def grow(part, pre, blocks):
        terms = [part[0]] + [swap(part[k], "heads", k) for k in range(1, planes)]
        return feed(chunk, terms, slope_of(pre), ups, blocks)

    first_terms = [parts[0][0]] + [swap(parts[0][k], "heads", k) for k in range(1, planes)]
    own_part, first_terms[2] = lax.optimization_barrier((own_parts[0], first_terms[2]))
    first_grown = feed(chunk, first_terms, slope_of(pres[0]), ups, far - 1)
    own_grown = grow(own_part, own_pre[0], 1)[0]
    grads, start = [], 0
    for part, pre, cut in zip(parts, pres, cuts):
        grown = first_grown if start == 0 else grow(part, pre, far - 1)
        blocks = [own_grown[start : start + cut]] + [grown[j] for j in range(far - 1)]
        start += cut
        own = sum(t.astype(F32) for t in scatter_terms(blocks, "seq", 2))
        blocks = [own[:, k * width : (k + 1) * width] for k in range(planes)]
        grads.append(
            blocks[0]
            + sum(swap(blocks[k].astype(BF16), "heads", k).astype(F32) for k in range(1, planes))
        )
    global_grad = state + jnp.concatenate(grads, 0)
    return (query_grad, global_grad)


def solution(mesh):
    placed = (
        P("seq", "heads"),
        P(None, "heads"),
        P(None, "heads"),
        P("seq", "heads"),
        P(None, "heads"),
        P(None, "heads"),
        P("seq", "heads"),
        P("heads", "seq"),
        P("seq", "heads"),
    )
    return jax.shard_map(
        local,
        mesh=mesh,
        in_specs=placed,
        out_specs=(P("seq", "heads"), P("seq", "heads")),
        check_vma=False,
    )
```
